128 devices in a mesh: grp: 4 (over y), col: 32 (over x, z, core).
Axes of the slice: x: 4, y: 4, z: 4, core: 2. Of those that a mesh axis runs over, the one named last changes fastest.
Arguments:
- tile_entries: bfloat16 [9216, 256, 256], P(('grp', 'col')), may hold values from -0.03125 to 0.03125
- slot_tile_row: int32 [9216], P(('grp', 'col')), may hold values from 0 to 15, as said below
- slot_tile_column: int32 [9216], P(('grp', 'col')), may hold values from 0 to 15
- tile_count: int32 [128], P(('grp', 'col')), may hold values from 24 to 72, as said below
- test_matrix: bfloat16 [131072, 320], P('col'), may hold values from -6 to 6
Outputs:
- basis: float32 [16384, 320], P(('grp', 'col'))
- projected: float32 [131072, 320], P('col')
The draws below stay inside these ranges and needn't reach their ends.
Inputs may be any that keep to these rules, and one draw needn't show every extreme that they name: Slots at or past a device's tile_count are not part of the matrix. The live slots of one device hold distinct (slot_tile_row, slot_tile_column) pairs. `tile_count`: some device has all 72 slots live.
All inputs are finite; a program needn't handle non-finite values.
Results may differ from the reference program's by a relative error of at most 0.0027.
Values may be sent and summed in bfloat16 or wider, within the bound.
A program may use at most 128 MiB of HBM per device.

```python
import jax
import jax.numpy as jnp
from jax import lax

TILE_EDGE = 256
K = 320
GROUP_TILE_ROWS = 16
SHARD_TILE_COLS = 16
DEVICE_CAPACITY = 72
TILES = 9216
NCOLS = 131072
N_GRP = 4
N_COL = 32


def device_tile_slots(key):
    key = jax.random.fold_in(key, 11)
    per_device_keys = jax.random.split(key, TILES // DEVICE_CAPACITY)
    picked_slots = jax.vmap(lambda single_key: jax.random.permutation(single_key, GROUP_TILE_ROWS * SHARD_TILE_COLS)[:DEVICE_CAPACITY])(per_device_keys)
    return picked_slots.reshape(-1).astype(jnp.int32)


def draw_slot_tile_row(key, part):
    return device_tile_slots(key) // SHARD_TILE_COLS


def draw_slot_tile_column(key, part):
    return device_tile_slots(key) % SHARD_TILE_COLS


def draw_tile_count(key, part):
    key = jax.random.fold_in(key, 23)
    count_key, full_key = jax.random.split(key)
    devices = TILES // DEVICE_CAPACITY
    counts = jax.random.randint(count_key, (devices,), DEVICE_CAPACITY // 3, DEVICE_CAPACITY + 1)
    full_device = jax.random.randint(full_key, (), 0, devices)
    return jnp.where(jnp.arange(devices) == full_device, DEVICE_CAPACITY, counts).astype(jnp.int32)


def block_scale(stream_key, extent, cuts, low, high):
    def one(position, shards_of):
        steps = jax.random.uniform(jax.random.fold_in(jax.random.fold_in(stream_key, 6), position), (shards_of,), jnp.float32, low / len(cuts), high / len(cuts))
        return jnp.repeat(jnp.exp(steps), extent[position] // shards_of).reshape((-1,) + (1,) * (len(extent) - position - 1))

    factor_of = one(*cuts[0])
    for cut in cuts[1:]:
        factor_of = factor_of * one(*cut)
    return factor_of


def bell_draw(own_key, extent, deviation, reach, pieces=(), kind=jnp.bfloat16):
    entries = deviation * jax.random.normal(own_key, extent, jnp.float32)
    if pieces:
        entries = entries * block_scale(own_key, extent, pieces, -0.22, 0.18)
    return jnp.clip(entries, -reach, reach).astype(kind)


def setup_inputs(seed: int = 0) -> dict:
    seeds = jax.random.split(jax.random.key(seed), 6)
    tile_entries = bell_draw(seeds[0], (TILES, TILE_EDGE, TILE_EDGE), (TILE_EDGE * N_COL * DEVICE_CAPACITY // GROUP_TILE_ROWS) ** -0.5, 0.03125, ((0, 128),))
    slot_tile_row = draw_slot_tile_row(jax.random.fold_in(seeds[5], 71), 0)
    slot_tile_column = draw_slot_tile_column(jax.random.fold_in(seeds[5], 71), 0)
    tile_count = draw_tile_count(jax.random.fold_in(seeds[5], 71), 0)
    test_matrix = bell_draw(seeds[4], (NCOLS, K), 1.0, 6.0, ((0, 32),))
    return dict(tile_entries=tile_entries, slot_tile_row=slot_tile_row, slot_tile_column=slot_tile_column, tile_count=tile_count, test_matrix=test_matrix)


def reference(tile_entries, slot_tile_row, slot_tile_column, tile_count, test_matrix):
    row_len = GROUP_TILE_ROWS * TILE_EDGE
    column_length = SHARD_TILE_COLS * TILE_EDGE
    total_rows = row_len * N_GRP
    zero_idx = jnp.int32(0)

    def place(tile_slot):
        device = tile_slot // DEVICE_CAPACITY
        group = device // N_COL
        shard = device % N_COL
        weight = jnp.where(tile_slot % DEVICE_CAPACITY < tile_count[device], 1.0, 0.0).astype(jnp.float32)
        row_start = (group * row_len + slot_tile_row[tile_slot] * TILE_EDGE).astype(jnp.int32)
        col_start = (shard * column_length + slot_tile_column[tile_slot] * TILE_EDGE).astype(jnp.int32)
        return (weight, row_start, col_start)

    def sample_step(running, tile_slot):
        weight, row_start, col_start = place(tile_slot)
        operand_block = lax.dynamic_slice(test_matrix, (col_start, zero_idx), (TILE_EDGE, K))
        product = jnp.dot(tile_entries[tile_slot].astype(jnp.float32), operand_block.astype(jnp.float32), preferred_element_type=jnp.float32) * weight
        former = lax.dynamic_slice(running, (row_start, zero_idx), (TILE_EDGE, K))
        return (lax.dynamic_update_slice(running, former + product, (row_start, zero_idx)), None)
    slots = jnp.arange(TILES, dtype=jnp.int32)
    sample = lax.scan(sample_step, jnp.zeros((total_rows, K), jnp.float32), slots)[0]
    gram = jnp.dot(sample.T, sample, precision=lax.Precision.HIGHEST) / total_rows
    lower = jnp.linalg.cholesky(gram)
    basis = jax.scipy.linalg.solve_triangular(lower, sample.T, lower=True).T
    basis_half = basis.astype(jnp.bfloat16)

    def project_step(running, tile_slot):
        weight, row_start, col_start = place(tile_slot)
        operand_block = lax.dynamic_slice(basis_half, (row_start, zero_idx), (TILE_EDGE, K))
        product = jnp.dot(tile_entries[tile_slot].T.astype(jnp.float32), operand_block.astype(jnp.float32), preferred_element_type=jnp.float32) * weight
        former = lax.dynamic_slice(running, (col_start, zero_idx), (TILE_EDGE, K))
        return (lax.dynamic_update_slice(running, former + product, (col_start, zero_idx)), None)
    projected = lax.scan(project_step, jnp.zeros((column_length * N_COL, K), jnp.float32), slots)[0]
    return (basis, projected)
```

```python
import functools

import jax
import jax.numpy as jnp
from jax import lax
from jax.experimental import pallas as pl
from jax.experimental.pallas import tpu as pltpu
from jax.sharding import PartitionSpec as P

MESH = pl.DeviceIdType.MESH
EDGE = 256
K = 320
HALF = 160
PART = 80
SLOTS = 72
GROUP = 8
NB = 16
BLK = 64
ROWS = 16384
F32 = jnp.float32
BF16 = jnp.bfloat16
I16 = jnp.int16
VMEM_LIMIT = 60 * 1024 * 1024
HIGHEST = lax.Precision.HIGHEST


def nn(a, b, **kw):
    return lax.dot_general(a, b, (((1,), (0,)), ((), ())), preferred_element_type=F32, **kw)


def nt(a, b, **kw):
    return lax.dot_general(a, b, (((1,), (1,)), ((), ())), preferred_element_type=F32, **kw)


def tn(a, b, **kw):
    return lax.dot_general(a, b, (((0,), (0,)), ((), ())), preferred_element_type=F32, **kw)


def scale_of(peak):
    top = jnp.maximum(jnp.max(peak, axis=1, keepdims=True), 1e-30)
    return top * (1.0 / 32767.0), 32767.0 / top


def encode(value, inverse):
    return jnp.round(value * inverse).astype(jnp.int32).astype(I16)


def decode(code, scale):
    return code.astype(jnp.int32).astype(F32) * scale


def pack(scale, first=0):
    lane = lax.broadcasted_iota(jnp.int32, (8, 128), 1)
    packed = jnp.zeros((8, 128), F32)
    for m in range(scale.shape[0] // 8):
        packed = jnp.where(lane == first + m, scale[8 * m : 8 * m + 8], packed)
    return packed


def unpack(packed, first, rows):
    return jnp.concatenate([packed[:, first + m : first + m + 1] for m in range(rows // 8)], axis=0)


def split(value):
    high = value.astype(BF16)
    return high, (value - high.astype(F32)).astype(BF16)


def finish_codes(acc, store, packed_ref):
    def peak_step(i, peak):
        block = jnp.abs(acc[i])
        return jnp.maximum(peak, jnp.maximum(block[:, :128], block[:, 128:]))

    peak = lax.fori_loop(0, NB, peak_step, jnp.zeros((K, 128), F32))
    scale, inverse = scale_of(peak)
    packed_ref[...] = pack(scale)

    def code_step(i, carry):
        store(i, encode(acc[i], inverse))
        return carry

    lax.fori_loop(0, NB, code_step, 0)


def sample_kernel(row_s, col_s, count_s, tiles, omega, codes, packed, omega_t, acc):
    step = pl.program_id(0)

    @pl.when(step == 0)
    def _():
        def flip(i, carry):
            omega_t[i] = omega[pl.ds(pl.multiple_of(i * EDGE, EDGE), EDGE), :].T
            acc[i] = jnp.zeros((K, EDGE), F32)
            return carry

        lax.fori_loop(0, NB, flip, 0)

    for u in range(GROUP):
        slot = step * GROUP + u
        row = jnp.where(slot < count_s[0], row_s[slot], NB)
        acc[row] += nt(omega_t[col_s[slot]], tiles[u])

    @pl.when(step == SLOTS // GROUP - 1)
    def _():
        def store(i, code):
            codes[i, 0] = code[:, :128]
            codes[i, 1] = code[:, 128:]

        finish_codes(acc, store, packed)


def project_kernel(row_s, col_s, count_s, tiles, s_codes, s_packed, codes, packed, s_split, acc):
    step = pl.program_id(0)

    @pl.when(step == 0)
    def _():
        def widen(i, carry):
            for core in range(2):
                high, low = split(decode(s_codes[i, core], unpack(s_packed[i, core], 0, K)))
                s_split[i, :K, core * 128 : core * 128 + 128] = high
                s_split[i, K:, core * 128 : core * 128 + 128] = low
            acc[i] = jnp.zeros((K, EDGE), F32)
            return carry

        lax.fori_loop(0, NB, widen, 0)

    for u in range(GROUP):
        slot = step * GROUP + u
        col = jnp.where(slot < count_s[0], col_s[slot], NB)
        both = nn(s_split[row_s[slot]], tiles[u])
        acc[col] += both[:K] + both[K:]

    @pl.when(step == SLOTS // GROUP - 1)
    def _():
        def store(i, code):
            codes[i] = code

        finish_codes(acc, store, packed)


def xor2(a, b):
    return (a % 2 + b % 2) % 2 + 2 * ((a // 2 + b // 2) % 2)


GENERATORS = (4, 12, 1, 3)


def span(generators):
    out = [0]
    for g in generators:
        out = out + [w ^ g for w in out]
    return out


def order_of(part):
    return GENERATORS[part:] + GENERATORS[:part]


def plane_kernel(
    codes, packed, share, out_codes, out_packed,
    pair_codes, pair_packed, total, *rest,
):
    sends, recvs = rest[0:4], rest[4:8]
    (
        send_packed, recv_packed, sem_pair, sem_rs_s, sem_rs_r, sem_rsp_s, sem_rsp_r,
        sem_ag_s, sem_ag_r, sem_agp_s, sem_agp_r, sem_fw_s, sem_fw_r, sem_fwp_s, sem_fwp_r,
    ) = rest[8:]
    me = lax.axis_index("col")
    chip, core = me // 2, me % 2
    x, z = chip // 4, chip % 4
    other = 1 - core

    def chip_at(w):
        return xor2(x, w // 4) * 4 + xor2(z, w % 4)

    sibling = chip * 2 + other
    peers = {g: chip_at(g) * 2 + core for g in GENERATORS}

    barrier = pltpu.get_barrier_semaphore()
    for peer in [sibling] + list(peers.values()):
        pl.semaphore_signal(barrier, inc=1, device_id={"col": peer}, device_id_type=MESH)
    pl.semaphore_wait(barrier, 5)

    def remote(src, dst, s, r, peer):
        copy = pltpu.make_async_remote_copy(
            src_ref=src, dst_ref=dst, send_sem=s, recv_sem=r,
            device_id={"col": peer}, device_id_type=MESH,
        )
        copy.start()
        return copy

    first = remote(codes.at[:, other], pair_codes, sem_pair.at[0], sem_pair.at[1], sibling)
    first_packed = remote(packed, pair_packed, sem_pair.at[2], sem_pair.at[3], sibling)
    own_scale = unpack(packed[...], 0, K)
    first_packed.wait()
    pair_scale = unpack(pair_packed[...], 0, K)
    first.wait()

    def join(w, carry):
        i = chip_at(w)
        total[w] = decode(codes[i, core], own_scale) + decode(pair_codes[i], pair_scale)
        return carry

    lax.fori_loop(0, NB, join, 0)

    started = {}

    def rs_send(part, t):
        gens = order_of(part)
        rows = slice(part * PART, part * PART + PART)
        blocks = [gens[t] ^ w for w in span(gens[t + 1 :])]
        peak = jnp.abs(total[blocks[0], rows])
        for w in blocks[1:]:
            peak = jnp.maximum(peak, jnp.abs(total[w, rows]))
        scale, inverse = scale_of(peak)
        send_packed[part, t] = pack(scale)
        for n, w in enumerate(blocks):
            sends[t][part, n] = encode(total[w, rows], inverse)
        started[part, t] = (
            remote(sends[t].at[part], recvs[t].at[part], sem_rs_s.at[part, t], sem_rs_r.at[part, t], peers[gens[t]]),
            remote(send_packed.at[part, t], recv_packed.at[part, t], sem_rsp_s.at[part, t], sem_rsp_r.at[part, t], peers[gens[t]]),
        )

    def rs_take(part, t):
        gens = order_of(part)
        rows = slice(part * PART, part * PART + PART)
        for copy in started[part, t]:
            copy.wait()
        scale = unpack(recv_packed[part, t], 0, PART)
        for n, w in enumerate(span(gens[t + 1 :])):
            total[w, rows] += decode(recvs[t][part, n], scale)

    for t in range(4):
        for part in range(4):
            if t > 0:
                rs_take(part, t - 1)
            rs_send(part, t)
    for part in range(4):
        rs_take(part, 3)

    mine = total[0]
    share[...] = mine
    scale, inverse = scale_of(jnp.abs(mine))
    out_codes[chip, core] = encode(mine, inverse)
    out_packed[chip, core] = pack(scale)

    pending = []

    def to_sibling(part, w):
        i = chip_at(w)
        rows = pl.ds(part * PART, PART)
        ref = out_codes.at[i, core, rows]
        pending.append(remote(ref, ref, sem_fw_s.at[part, w], sem_fw_r.at[part, w], sibling))
        if part == 0:
            ref = out_packed.at[i, core]
            pending.append(remote(ref, ref, sem_fwp_s.at[w], sem_fwp_r.at[w], sibling))

    gather = {}
    for t in range(4):
        for part in range(4):
            gens = order_of(part)
            rows = pl.ds(part * PART, PART)
            held = span(gens[:t])
            if t > 0:
                for copy in gather[part, t - 1]:
                    copy.wait()
            gather[part, t] = []
            for w in held:
                i = chip_at(w)
                ref = out_codes.at[i, core, rows]
                got = w ^ gens[t]
                gather[part, t].append(
                    remote(ref, ref, sem_ag_s.at[part, got], sem_ag_r.at[part, got], peers[gens[t]])
                )
                if part == 0:
                    ref = out_packed.at[i, core]
                    gather[part, t].append(
                        remote(ref, ref, sem_agp_s.at[got], sem_agp_r.at[got], peers[gens[t]])
                    )
            for w in held[len(held) // 2 :] if t > 0 else held:
                to_sibling(part, w)
    for part in range(4):
        gens = order_of(part)
        for copy in gather[part, 3]:
            copy.wait()
        held = span(gens)
        for w in held[8:]:
            to_sibling(part, w)
    for copy in pending:
        copy.wait()


def pivot_block(block):
    n = BLK // 8
    eye = (
        lax.broadcasted_iota(jnp.int32, (BLK, BLK), 0) == lax.broadcasted_iota(jnp.int32, (BLK, BLK), 1)
    ).astype(F32)
    whole = jnp.concatenate([block, eye], axis=1)
    parts = [whole[8 * g : 8 * g + 8] for g in range(n)]
    sub = lax.broadcasted_iota(jnp.int32, (8, 128), 0)
    for k in range(0, BLK, 4):
        home, at = k // 8, k % 8
        cols = [
            [jnp.broadcast_to(parts[g][:, k + i : k + i + 1], (8, 128)) for g in range(home, n)] for i in range(4)
        ]
        rows = [parts[home][at + i : at + i + 1] for i in range(4)]
        steps = []
        roots = []
        for i in range(4):
            pivot = cols[i][0][at + i : at + i + 1]
            inverse = 1.0 / pivot
            roots.append(lax.rsqrt(pivot))
            steps.append(rows[i] * inverse)
            for j in range(i + 1, 4):
                rows[j] = rows[j] - cols[i][0][at + j : at + j + 1] * steps[i]
                factor = cols[j][0][at + i : at + i + 1] * inverse
                cols[j] = [c - b * factor for c, b in zip(cols[j], cols[i])]
        for g in range(home, n):
            new = parts[g]
            for i in range(4):
                new = new - cols[i][g - home] * steps[i]
            if g == home:
                new = jnp.where(sub > at + 3, new, parts[g])
                for i in range(4):
                    new = jnp.where(sub == at + i, rows[i] * roots[i], new)
            parts[g] = new
    return jnp.concatenate(parts, axis=0)[:, BLK:]


def ring_kernel(
    codes, packed, s_codes, s_packed, out_codes, out_packed, factor,
    first_in, second_in, third_in, third_out, sums, near_packed, third_packed_in, third_packed_out,
    high, low, gram_parts, gram_all, work,
    sem_a_s, sem_a_r, sem_p_s, sem_p_r, sem_c_s, sem_c_r, sem_cp_s, sem_cp_r,
    sem_g_s, sem_g_r, sem_gp_s, sem_gp_r, sem_y_s, sem_y_r, sem_w_s, sem_w_r,
):
    y = lax.axis_index("grp")
    me = lax.axis_index("col")
    near = (xor2(y, 1), xor2(y, 3))

    barrier = pltpu.get_barrier_semaphore()
    for d in range(1, 4):
        pl.semaphore_signal(barrier, inc=1, device_id={"grp": (y + d) % 4}, device_id_type=MESH)

    def greet(d, carry):
        pl.semaphore_signal(barrier, inc=1, device_id={"col": (me + d) % 32}, device_id_type=MESH)
        return carry

    lax.fori_loop(1, 32, greet, 0)
    pl.semaphore_wait(barrier, 34)

    def remote(src, dst, s, r, axis, peer):
        copy = pltpu.make_async_remote_copy(
            src_ref=src, dst_ref=dst, send_sem=s, recv_sem=r,
            device_id={axis: peer}, device_id_type=MESH,
        )
        copy.start()
        return copy

    def quarter(w):
        return pl.ds(pl.multiple_of(4 * xor2(y, w), 4), 4)

    gens = ((1, 3), (3, 1))
    ends = [pl.ds(h * HALF, HALF) for h in range(2)]
    line = {1: 0, 3: 1}

    scales = [remote(packed, near_packed.at[n], sem_p_s.at[n], sem_p_r.at[n], "grp", near[n]) for n in range(2)]
    first, second = [], []
    for h in range(2):
        g, g2 = gens[h]
        first.append(
            remote(codes.at[quarter(2), ends[h]], first_in.at[h], sem_a_s.at[h, 0], sem_a_r.at[h, 0], "grp", near[line[g]])
        )
    for h in range(2):
        g, g2 = gens[h]
        second.append(
            remote(codes.at[quarter(g), ends[h]], second_in.at[h], sem_a_s.at[h, 1], sem_a_r.at[h, 1], "grp", near[line[g]])
        )

    def widen(i, carry):
        for core in range(2):
            lanes = slice(core * 128, core * 128 + 128)
            a, b = split(decode(s_codes[i, core], unpack(s_packed[i, core], 0, K)))
            high[i, :K, lanes] = a
            low[i, :K, lanes] = b
        high[i, K:] = jnp.zeros((64, EDGE), BF16)
        low[i, K:] = jnp.zeros((64, EDGE), BF16)
        return carry

    lax.fori_loop(0, NB, widen, 0)
    block = me % 30
    rows = pl.ds(pl.multiple_of(32 * (block // 3), 32), 32)
    cols = pl.ds(pl.multiple_of(128 * (block % 3), 128), 128)

    def gram_step(i, acc):
        a, b = high[i, rows], low[i, rows]
        c, d = high[i, cols], low[i, cols]
        return acc + (nt(a, c) + (nt(a, d) + nt(b, c)))

    gram_parts[y] = lax.fori_loop(0, NB, gram_step, jnp.zeros((32, 128), F32))
    over_y = [
        remote(gram_parts.at[y], gram_parts.at[y], sem_y_s.at[d], sem_y_r.at[d], "grp", (y + d) % 4) for d in range(1, 4)
    ]

    for copy in scales:
        copy.wait()
    own_scale = unpack(packed[...], 0, K)

    def summed(h, w, takes, target):
        at = 4 * xor2(y, w)

        def body(j, peak):
            value = decode(codes[at + j, ends[h]], own_scale[h * HALF : h * HALF + HALF])
            for ref, scale in takes:
                value = value + decode(ref[h, j], scale)
            target[h, j] = value
            value = jnp.abs(value)
            return jnp.maximum(peak, jnp.maximum(value[:, :128], value[:, 128:]))

        return lax.fori_loop(0, 4, body, jnp.zeros((HALF, 128), F32))

    near_scale = []
    third = []
    for h in range(2):
        g, g2 = gens[h]
        near_scale.append(unpack(near_packed[line[g]], 20 * h, HALF))
        first[h].wait()
        scale, inverse = scale_of(summed(h, g2, [(first_in, near_scale[h])], sums))
        third_packed_out[h] = pack(scale)

        def code(j, carry):
            third_out[h, j] = encode(sums[h, j], inverse)
            return carry

        lax.fori_loop(0, 4, code, 0)
        third.append(
            (
                remote(third_packed_out.at[h], third_packed_in.at[h], sem_cp_s.at[h], sem_cp_r.at[h], "grp", near[line[g2]]),
                remote(third_out.at[h], third_in.at[h], sem_c_s.at[h], sem_c_r.at[h], "grp", near[line[g2]]),
            )
        )

    for copy in over_y:
        copy.wait()
    gram_all[me] = (gram_parts[0] + gram_parts[1]) + (gram_parts[2] + gram_parts[3])

    def spread(d):
        return pltpu.make_async_remote_copy(
            src_ref=gram_all.at[me], dst_ref=gram_all.at[me], send_sem=sem_w_s.at[d], recv_sem=sem_w_r.at[d],
            device_id={"col": (me + d) % 32}, device_id_type=MESH,
        )

    def spread_start(d, carry):
        spread(d).start()
        return carry

    def spread_wait(d, carry):
        spread(d).wait()
        return carry

    lax.fori_loop(1, 32, spread_start, 0)
    lax.fori_loop(1, 32, spread_wait, 0)

    for r in range(10):
        for c in range(3):
            work[32 * r : 32 * r + 32, 128 * c : 128 * c + 128] = gram_all[3 * r + c] * (1.0 / ROWS)
    work[:, 384:] = (
        lax.broadcasted_iota(jnp.int32, (K, 384), 0) == lax.broadcasted_iota(jnp.int32, (K, 384), 1)
    ).astype(F32)

    def eliminate(b):
        top, low_row = b * BLK, b * BLK + BLK
        inverse = pivot_block(work[top:low_row, top:low_row])
        panel = nn(inverse, work[top:low_row, :], precision=HIGHEST)
        work[top:low_row, :] = panel
        if low_row < K:
            left = panel[:, low_row:K]
            lane = low_row // 128 * 128
            work[low_row:, lane:384] -= tn(left, panel[:, lane:384], precision=HIGHEST)
            edge = 384 + (low_row + 127) // 128 * 128
            work[low_row:, 384:edge] -= tn(left, panel[:, 384:edge], precision=HIGHEST)

    gather, gather_packed = {}, {}

    def share_out(h):
        g, g2 = gens[h]
        second[h].wait()
        for copy in third[h]:
            copy.wait()
        third_scale = unpack(third_packed_in[h], 0, HALF)
        scale, inverse = scale_of(summed(h, 0, [(second_in, near_scale[h]), (third_in, third_scale)], sums))
        out_packed[y, h] = pack(scale)

        def code(j, carry):
            out_codes[4 * y + j, ends[h]] = encode(sums[h, j], inverse)
            return carry

        lax.fori_loop(0, 4, code, 0)
        send_quarter(h, 0, g2, 0)
        send_quarter(h, 0, g, 1)

    def send_quarter(h, w, g, n):
        ref = out_codes.at[quarter(w), ends[h]]
        gather[h, n] = remote(ref, ref, sem_g_s.at[h, n], sem_g_r.at[h, n], "grp", near[line[g]])
        ref = out_packed.at[xor2(y, w), h]
        gather_packed[h, n] = remote(ref, ref, sem_gp_s.at[h, n], sem_gp_r.at[h, n], "grp", near[line[g]])

    def pass_on(h):
        g, g2 = gens[h]
        gather[h, 0].wait()
        gather_packed[h, 0].wait()
        send_quarter(h, g2, g, 2)

    eliminate(0)
    for h in range(2):
        share_out(h)
    eliminate(1)
    eliminate(2)
    for h in range(2):
        pass_on(h)
    eliminate(3)
    eliminate(4)
    factor[...] = work[:, 384:]
    for h in range(2):
        for n in (1, 2):
            gather[h, n].wait()
            gather_packed[h, n].wait()


def final_kernel(codes, packed, share, factor, projected, basis, w_high, w_low):
    step = pl.program_id(0)

    @pl.when(step == 0)
    def _():
        w = factor[:, :K]
        a, b = split(w)
        w_high[...] = a
        w_low[...] = b
        basis[...] = nt(share[...].T, w, precision=HIGHEST)

    q = step // 2
    scale = jnp.concatenate([unpack(packed[q, 0], 0, HALF), unpack(packed[q, 1], 0, HALF)], axis=0)
    for j in range(2):
        a, b = split(decode(codes[j], scale).T)
        projected[EDGE * j : EDGE * j + EDGE, :] = nt(a, w_high[...]) + (nt(a, w_low[...]) + nt(b, w_high[...]))


def whole(shape):
    return pl.BlockSpec(shape, lambda *_: (0,) * len(shape))


def vmem(n):
    return [pl.BlockSpec(memory_space=pltpu.VMEM)] * n


def shape(dims, dtype):
    return jax.ShapeDtypeStruct(dims, dtype)


def local(tile_entries, slot_tile_row, slot_tile_column, tile_count, test_matrix):
    tiles_spec = pl.BlockSpec((GROUP, EDGE, EDGE), lambda i, *_: (i, 0, 0))
    scalars = (slot_tile_row, slot_tile_column, tile_count)
    params = pltpu.CompilerParams(vmem_limit_bytes=VMEM_LIMIT)

    codes, packed = pl.pallas_call(
        sample_kernel,
        grid_spec=pltpu.PrefetchScalarGridSpec(
            num_scalar_prefetch=3,
            grid=(SLOTS // GROUP,),
            in_specs=[tiles_spec, whole((NB * EDGE, K))],
            out_specs=[whole((NB, 2, K, 128)), whole((8, 128))],
            scratch_shapes=[pltpu.VMEM((NB, K, EDGE), BF16), pltpu.VMEM((NB + 1, K, EDGE), F32)],
        ),
        out_shape=[shape((NB, 2, K, 128), I16), shape((8, 128), F32)],
        compiler_params=params,
        name="sample",
    )(*scalars, tile_entries, test_matrix)

    dma = pltpu.SemaphoreType.DMA
    share, s_codes, s_packed = pl.pallas_call(
        plane_kernel,
        in_specs=vmem(2),
        out_specs=vmem(3),
        out_shape=[shape((K, 128), F32), shape((NB, 2, K, 128), I16), shape((NB, 2, 8, 128), F32)],
        scratch_shapes=[
            pltpu.VMEM((NB, K, 128), I16),
            pltpu.VMEM((8, 128), F32),
            pltpu.VMEM((NB, K, 128), F32),
        ]
        + [pltpu.VMEM((4, n, PART, 128), I16) for n in (8, 4, 2, 1)] * 2
        + [
            pltpu.VMEM((4, 4, 8, 128), F32),
            pltpu.VMEM((4, 4, 8, 128), F32),
            dma((4,)),
            dma((4, 4)), dma((4, 4)), dma((4, 4)), dma((4, 4)),
            dma((4, 16)), dma((4, 16)), dma((16,)), dma((16,)),
            dma((4, 16)), dma((4, 16)), dma((16,)), dma((16,)),
        ],
        compiler_params=pltpu.CompilerParams(
            vmem_limit_bytes=VMEM_LIMIT, collective_id=0, has_side_effects=True
        ),
        name="plane_sum",
    )(codes, packed)

    p_codes, p_packed = pl.pallas_call(
        project_kernel,
        grid_spec=pltpu.PrefetchScalarGridSpec(
            num_scalar_prefetch=3,
            grid=(SLOTS // GROUP,),
            in_specs=[tiles_spec, whole((NB, 2, K, 128)), whole((NB, 2, 8, 128))],
            out_specs=[whole((NB, K, EDGE)), whole((8, 128))],
            scratch_shapes=[pltpu.VMEM((NB, 2 * K, EDGE), BF16), pltpu.VMEM((NB + 1, K, EDGE), F32)],
        ),
        out_shape=[shape((NB, K, EDGE), I16), shape((8, 128), F32)],
        compiler_params=params,
        name="project",
    )(*scalars, tile_entries, s_codes, s_packed)

    block_in = pltpu.VMEM((2, 4, HALF, EDGE), I16)
    out_codes, out_packed, factor = pl.pallas_call(
        ring_kernel,
        in_specs=vmem(4),
        out_specs=vmem(3),
        out_shape=[shape((NB, K, EDGE), I16), shape((4, 2, 8, 128), F32), shape((K, 384), F32)],
        scratch_shapes=[
            block_in, block_in, block_in, block_in,
            pltpu.VMEM((2, 4, HALF, EDGE), F32),
            pltpu.VMEM((2, 8, 128), F32),
            pltpu.VMEM((2, 8, 128), F32),
            pltpu.VMEM((2, 8, 128), F32),
            pltpu.VMEM((NB, 384, EDGE), BF16),
            pltpu.VMEM((NB, 384, EDGE), BF16),
            pltpu.VMEM((4, 32, 128), F32),
            pltpu.VMEM((32, 32, 128), F32),
            pltpu.VMEM((K, 768), F32),
            dma((2, 2)), dma((2, 2)), dma((2,)), dma((2,)),
            dma((2,)), dma((2,)), dma((2,)), dma((2,)),
            dma((2, 3)), dma((2, 3)), dma((2, 3)), dma((2, 3)),
            dma((4,)), dma((4,)), dma((32,)), dma((32,)),
        ],
        compiler_params=pltpu.CompilerParams(
            vmem_limit_bytes=VMEM_LIMIT, collective_id=1, has_side_effects=True
        ),
        name="ring_sum",
    )(p_codes, p_packed, s_codes, s_packed)

    projected, basis = pl.pallas_call(
        final_kernel,
        grid=(8,),
        in_specs=[
            pl.BlockSpec((2, K, EDGE), lambda i: (i, 0, 0)),
            whole((4, 2, 8, 128)), whole((K, 128)), whole((K, 384)),
        ],
        out_specs=[pl.BlockSpec((2 * EDGE, K), lambda i: (i, 0)), whole((128, K))],
        out_shape=[shape((NB * EDGE, K), F32), shape((128, K), F32)],
        scratch_shapes=[pltpu.VMEM((K, K), BF16), pltpu.VMEM((K, K), BF16)],
        compiler_params=params,
        name="final",
    )(out_codes, out_packed, share, factor)
    return (basis, projected)


def solution(mesh):
    placed = (
        P(("grp", "col"), None, None),
        P(("grp", "col")),
        P(("grp", "col")),
        P(("grp", "col")),
        P("col", None),
    )
    return jax.shard_map(
        local,
        mesh=mesh,
        in_specs=placed,
        out_specs=(P(("grp", "col"), None), P("col", None)),
        check_vma=False,
    )
```

```python
import functools

import jax
import jax.numpy as jnp
from jax import lax
from jax.experimental import pallas as pl
from jax.experimental.pallas import tpu as pltpu
from jax.sharding import PartitionSpec as P

MESH = pl.DeviceIdType.MESH
EDGE = 256
K = 320
HALF = 160
PART = 80
SLOTS = 72
GROUP = 8
GROUPS = SLOTS // GROUP
NB = 16
BLK = 64
ROWS = 16384
FCOLS = 4
FSTEPS = NB // FCOLS
F32 = jnp.float32
BF16 = jnp.bfloat16
I16 = jnp.int16
VMEM_LIMIT = 60 * 1024 * 1024
HIGHEST = lax.Precision.HIGHEST


def nn(a, b, **kw):
    return lax.dot_general(a, b, (((1,), (0,)), ((), ())), preferred_element_type=F32, **kw)


def nt(a, b, **kw):
    return lax.dot_general(a, b, (((1,), (1,)), ((), ())), preferred_element_type=F32, **kw)


def tn(a, b, **kw):
    return lax.dot_general(a, b, (((0,), (0,)), ((), ())), preferred_element_type=F32, **kw)


def scale_of(peak):
    top = jnp.maximum(jnp.max(peak, axis=1, keepdims=True), 1e-30)
    return top * (1.0 / 32767.0), 32767.0 / top


def encode(value, inverse):
    return jnp.round(value * inverse).astype(jnp.int32).astype(I16)


def decode(code, scale):
    return code.astype(jnp.int32).astype(F32) * scale


def pack(scale, first=0):
    lane = lax.broadcasted_iota(jnp.int32, (8, 128), 1)
    packed = jnp.zeros((8, 128), F32)
    for m in range(scale.shape[0] // 8):
        packed = jnp.where(lane == first + m, scale[8 * m : 8 * m + 8], packed)
    return packed


def unpack(packed, first, rows):
    return jnp.concatenate([packed[:, first + m : first + m + 1] for m in range(rows // 8)], axis=0)


def split(value):
    high = value.astype(BF16)
    return high, (value - high.astype(F32)).astype(BF16)


def sample_kernel(
    row_s, col_s, count_s, tiles_hbm, omega_hbm,
    codes, packed, order, order_row, start,
    tiles, omega, acc, fill, sems,
):
    load_omega = pltpu.make_async_copy(omega_hbm, omega, sems.at[GROUPS])
    load_omega.start()
    loads = []
    for n in range(GROUPS):
        part = pl.ds(n * GROUP, GROUP)
        loads.append(pltpu.make_async_copy(tiles_hbm.at[part], tiles.at[part], sems.at[n]))
        loads[-1].start()

    def clear(i, carry):
        acc[i] = jnp.zeros((K, EDGE), F32)
        return carry

    lax.fori_loop(0, NB, clear, 0)

    def bin_of(slot):
        return jnp.where(slot < count_s[0], col_s[slot], NB)

    for c in range(NB + 1):
        fill[c] = 0

    def count(slot, carry):
        c = bin_of(slot)
        fill[c] = fill[c] + 1
        return carry

    lax.fori_loop(0, SLOTS, count, 0)
    begin = jnp.int32(0)
    for c in range(NB + 1):
        start[c] = begin
        size = fill[c]
        fill[c] = begin
        begin = begin + size

    def put(slot, carry):
        c = bin_of(slot)
        at = fill[c]
        fill[c] = at + 1
        order[at] = slot
        order_row[at] = row_s[slot]
        return carry

    lax.fori_loop(0, SLOTS, put, 0)

    load_omega.wait()
    for n in range(GROUPS):
        loads[n].wait()
        for u in range(GROUP):
            slot = n * GROUP + u
            row = jnp.where(slot < count_s[0], row_s[slot], NB)
            left = omega[:, pl.ds(pl.multiple_of(col_s[slot] * EDGE, EDGE), EDGE)]
            acc[row] += nt(left, tiles[slot])

    def peak_step(i, peak):
        block = jnp.abs(acc[i])
        return jnp.maximum(peak, jnp.maximum(block[:, :128], block[:, 128:]))

    scale, inverse = scale_of(lax.fori_loop(0, NB, peak_step, jnp.zeros((K, 128), F32)))
    packed[...] = pack(scale)

    def code_step(i, carry):
        code = encode(acc[i], inverse)
        for ch in range(2):
            for core in range(2):
                codes[ch, i, core] = code[ch * HALF : ch * HALF + HALF, core * 128 : core * 128 + 128]
        return carry

    lax.fori_loop(0, NB, code_step, 0)


def xor2(a, b):
    return (a % 2 + b % 2) % 2 + 2 * ((a // 2 + b // 2) % 2)


def pivot_block(block):
    n = BLK // 8
    eye = (
        lax.broadcasted_iota(jnp.int32, (BLK, BLK), 0) == lax.broadcasted_iota(jnp.int32, (BLK, BLK), 1)
    ).astype(F32)
    whole = jnp.concatenate([block, eye], axis=1)
    parts = [whole[8 * g : 8 * g + 8] for g in range(n)]
    sub = lax.broadcasted_iota(jnp.int32, (8, 128), 0)
    for k in range(0, BLK, 4):
        home, at = k // 8, k % 8
        cols = [
            [jnp.broadcast_to(parts[g][:, k + i : k + i + 1], (8, 128)) for g in range(home, n)] for i in range(4)
        ]
        rows = [parts[home][at + i : at + i + 1] for i in range(4)]
        steps = []
        roots = []
        for i in range(4):
            pivot = cols[i][0][at + i : at + i + 1]
            inverse = 1.0 / pivot
            roots.append(lax.rsqrt(pivot))
            steps.append(rows[i] * inverse)
            for j in range(i + 1, 4):
                rows[j] = rows[j] - cols[i][0][at + j : at + j + 1] * steps[i]
                factor = cols[j][0][at + i : at + i + 1] * inverse
                cols[j] = [c - b * factor for c, b in zip(cols[j], cols[i])]
        for g in range(home, n):
            new = parts[g]
            for i in range(4):
                new = new - cols[i][g - home] * steps[i]
            if g == home:
                new = jnp.where(sub > at + 3, new, parts[g])
                for i in range(4):
                    new = jnp.where(sub == at + i, rows[i] * roots[i], new)
            parts[g] = new
    return jnp.concatenate(parts, axis=0)[:, BLK:]

def main_kernel(
    order, order_row, start, codes, packed, tiles_hbm,
    share, out_codes, out_packed, factor,
    pair_codes, pair_packed, total, sb, rb, sc, rc, sbp, rbp, scp, rcp, gat, gat_packed,
    s_split, tiles, prefix, p_codes, p_packed,
    first_in, second_in, third_in, third_out, sums, near_packed, third_packed_in, third_packed_out,
    gram_parts, gram_all, work,
    sem_t, sem_pair, sem_b, sem_c, sem_g1, sem_g2, sem_gp1, sem_gp2, sem_f, sem_fp,
    sem_a, sem_p, sem_3, sem_3p, sem_g, sem_gp, sem_y, sem_w,
):
    y = lax.axis_index("grp")
    me = lax.axis_index("col")
    chip, core = me // 2, me % 2
    x, z = chip // 4, chip % 4
    other = 1 - core
    sibling = {"col": chip * 2 + other}

    def along_x(d):
        return {"col": (xor2(x, d) * 4 + z) * 2 + core}

    def along_z(d):
        return {"col": (x * 4 + xor2(z, d)) * 2 + core}

    def along_y(d):
        return {"grp": xor2(y, d)}

    load_tiles = pltpu.make_async_copy(tiles_hbm, tiles, sem_t)
    load_tiles.start()

    barrier = pltpu.get_barrier_semaphore()
    greeted = [sibling] + [f(d) for f in (along_x, along_z, along_y) for d in (1, 2, 3)]
    for peer in greeted:
        pl.semaphore_signal(barrier, inc=1, device_id=peer, device_id_type=MESH)
    pl.semaphore_wait(barrier, len(greeted))

    def remote(src, dst, sems, peer):
        copy = pltpu.make_async_remote_copy(
            src_ref=src, dst_ref=dst, send_sem=sems.at[0], recv_sem=sems.at[1],
            device_id=peer, device_id_type=MESH,
        )
        copy.start()
        return copy

    pair = {
        ch: remote(codes.at[ch, :, other], pair_codes.at[ch], sem_pair.at[ch], sibling) for ch in range(2)
    }
    pair_scales = remote(packed, pair_packed, sem_pair.at[2], sibling)
    pair_scales.wait()

    def join(ch):
        pair[ch].wait()
        own_scale = unpack(packed[...], 20 * ch, HALF)
        pair_scale = unpack(pair_packed[...], 20 * ch, HALF)

        def body(w, carry):
            i = xor2(x, w // 4) * 4 + xor2(z, w % 4)
            total[ch, w] = decode(codes[ch, i, core], own_scale) + decode(pair_codes[ch, i], pair_scale)
            return carry

        lax.fori_loop(0, NB, body, 0)

    def block(p, a, b):
        return 4 * a + b if p == 0 else 4 * b + a

    outer = (along_x, along_z)
    inner = (along_z, along_x)
    part_rows = [slice(p * PART, p * PART + PART) for p in range(2)]
    part_at = [pl.ds(p * PART, PART) for p in range(2)]
    flying = {}

    def b_send(ch):
        for p in range(2):
            peak = jnp.zeros((PART, 128), F32)
            for d in range(1, 4):
                for e in range(4):
                    peak = jnp.maximum(peak, jnp.abs(total[ch, block(p, d, e), part_rows[p]]))
            scale, inverse = scale_of(peak)
            sbp[ch, p] = pack(scale)
            flying["b", ch, p] = []
            for d in range(1, 4):
                for e in range(4):
                    sb[ch, p, d - 1, e] = encode(total[ch, block(p, d, e), part_rows[p]], inverse)
                flying["b", ch, p] += [
                    remote(sb.at[ch, p, d - 1], rb.at[ch, p, d - 1], sem_b.at[ch, p, d - 1], outer[p](d)),
                    remote(sbp.at[ch, p], rbp.at[ch, p, d - 1], sem_b.at[ch, p, d + 2], outer[p](d)),
                ]

    def b_take(ch):
        for p in range(2):
            for copy in flying["b", ch, p]:
                copy.wait()
            scales = [unpack(rbp[ch, p, d], 0, PART) for d in range(3)]
            peak = jnp.zeros((PART, 128), F32)
            for e in range(4):
                at = block(p, 0, e)
                value = total[ch, at, part_rows[p]]
                for d in range(3):
                    value = value + decode(rb[ch, p, d, e], scales[d])
                total[ch, at, part_rows[p]] = value
                if e > 0:
                    peak = jnp.maximum(peak, jnp.abs(value))
            scale, inverse = scale_of(peak)
            scp[ch, p] = pack(scale)
            flying["c", ch, p] = []
            for e in range(1, 4):
                sc[ch, p, e - 1] = encode(total[ch, block(p, 0, e), part_rows[p]], inverse)
                flying["c", ch, p] += [
                    remote(sc.at[ch, p, e - 1], rc.at[ch, p, e - 1], sem_c.at[ch, p, e - 1], inner[p](e)),
                    remote(scp.at[ch, p], rcp.at[ch, p, e - 1], sem_c.at[ch, p, e + 2], inner[p](e)),
                ]

    def c_take(ch):
        for p in range(2):
            for copy in flying["c", ch, p]:
                copy.wait()
            value = total[ch, 0, part_rows[p]]
            for e in range(3):
                value = value + decode(rc[ch, p, e], unpack(rcp[ch, p, e], 0, PART))
            share[ch * HALF + p * PART : ch * HALF + p * PART + PART, :] = value
        mine = share[ch * HALF : ch * HALF + HALF, :]
        scale, inverse = scale_of(jnp.abs(mine))
        gat[ch, x, z, core] = encode(mine, inverse)
        gat_packed[ch, x, z, core] = pack(scale)
        flying["g1", ch] = []
        for d in range(1, 4):
            for p in range(2):
                ref = gat.at[ch, x, z, core, part_at[p]]
                flying["g1", ch].append(remote(ref, ref, sem_g1.at[ch, p, d], inner[p](d)))
            ref = gat_packed.at[ch, x, z, core]
            flying["g1", ch].append(remote(ref, ref, sem_gp1.at[ch, d], inner[0](d)))

    def g1_take(ch):
        for copy in flying["g1", ch]:
            copy.wait()
        flying["g2", ch] = []
        for d in range(1, 4):
            ref = gat.at[ch, x, :, core, part_at[0]]
            flying["g2", ch].append(remote(ref, ref, sem_g2.at[ch, 0, d], along_x(d)))
            ref = gat.at[ch, :, z, core, part_at[1]]
            flying["g2", ch].append(remote(ref, ref, sem_g2.at[ch, 1, d], along_z(d)))
            ref = gat_packed.at[ch, x, :, core]
            flying["g2", ch].append(remote(ref, ref, sem_gp2.at[ch, d], along_x(d)))

    def g2_take(ch):
        for copy in flying["g2", ch]:
            copy.wait()
        ref, packed_ref = gat.at[ch, :, :, core], gat_packed.at[ch, :, :, core]
        flying["f", ch] = [
            remote(ref, ref, sem_f.at[ch], sibling),
            remote(packed_ref, packed_ref, sem_fp.at[ch], sibling),
        ]

    def widen(ch):
        for copy in flying["f", ch]:
            copy.wait()

        def body(i, carry):
            for c in range(2):
                lanes = slice(c * 128, c * 128 + 128)
                scale = unpack(gat_packed[ch, i // 4, i % 4, c], 0, HALF)
                high, low = split(decode(gat[ch, i // 4, i % 4, c], scale))
                s_split[ch, i, :HALF, lanes] = high
                s_split[ch, i, HALF:, lanes] = low
            return carry

        lax.fori_loop(0, NB, body, 0)

    def project(ch):
        prefix[0] = jnp.zeros((HALF, EDGE), F32)

        def body(m, carry):
            for u in range(GROUP):
                n = m * GROUP + u
                both = nn(s_split[ch, order_row[n]], tiles[order[n]])
                prefix[n + 1] = prefix[n] + (both[:HALF] + both[HALF:])
            return carry

        lax.fori_loop(0, GROUPS, body, 0)

        def value_of(j):
            return prefix[start[j + 1]] - prefix[start[j]]

        def peak_step(j, peak):
            value = jnp.abs(value_of(j))
            return jnp.maximum(peak, jnp.maximum(value[:, :128], value[:, 128:]))

        scale, inverse = scale_of(lax.fori_loop(0, NB, peak_step, jnp.zeros((HALF, 128), F32)))
        p_packed[ch] = pack(scale)

        def code_step(j, carry):
            p_codes[ch, j] = encode(value_of(j), inverse)
            return carry

        lax.fori_loop(0, NB, code_step, 0)

    gens = ((1, 3), (3, 1))
    line = {1: 0, 3: 1}

    def quarter(w):
        return pl.ds(pl.multiple_of(4 * xor2(y, w), 4), 4)

    def y_send(ch):
        flying["p", ch] = [
            remote(p_packed.at[ch], near_packed.at[ch, n], sem_p.at[ch, n], along_y(g)) for n, g in enumerate((1, 3))
        ]
        for n, target in ((0, first_in), (1, second_in)):
            for h in range(2):
                g, g2 = gens[h]
                w = (2, g)[n]
                flying["a", ch, h, n] = remote(
                    p_codes.at[ch, quarter(w), part_at[h]], target.at[ch, h], sem_a.at[ch, h, n], along_y(g)
                )

    def summed(ch, h, w, takes):
        at = 4 * xor2(y, w)
        own_scale = unpack(p_packed[ch], 10 * h, PART)

        def body(j, peak):
            value = decode(p_codes[ch, at + j, part_rows[h]], own_scale)
            for ref, scale in takes:
                value = value + decode(ref[ch, h, j], scale)
            sums[j] = value
            value = jnp.abs(value)
            return jnp.maximum(peak, jnp.maximum(value[:, :128], value[:, 128:]))

        return lax.fori_loop(0, 4, body, jnp.zeros((PART, 128), F32))

    def near_scale(ch, h):
        return unpack(near_packed[ch, line[gens[h][0]]], 10 * h, PART)

    def y_third(ch):
        for copy in flying["p", ch]:
            copy.wait()
        for h in range(2):
            g, g2 = gens[h]
            flying["a", ch, h, 0].wait()
            scale, inverse = scale_of(summed(ch, h, g2, [(first_in, near_scale(ch, h))]))
            third_packed_out[ch, h] = pack(scale)

            def code(j, carry):
                third_out[ch, h, j] = encode(sums[j], inverse)
                return carry

            lax.fori_loop(0, 4, code, 0)
            flying["3", ch, h] = [
                remote(third_packed_out.at[ch, h], third_packed_in.at[ch, h], sem_3p.at[ch, h], along_y(g2)),
                remote(third_out.at[ch, h], third_in.at[ch, h], sem_3.at[ch, h], along_y(g2)),
            ]

    def send_quarter(ch, h, w, g, n):
        ref = out_codes.at[ch, quarter(w), part_at[h]]
        packed_ref = out_packed.at[xor2(y, w), ch, h]
        flying["q", ch, h, n] = [
            remote(ref, ref, sem_g.at[ch, h, n], along_y(g)),
            remote(packed_ref, packed_ref, sem_gp.at[ch, h, n], along_y(g)),
        ]

    def y_share(ch):
        for h in range(2):
            g, g2 = gens[h]
            flying["a", ch, h, 1].wait()
            for copy in flying["3", ch, h]:
                copy.wait()
            third_scale = unpack(third_packed_in[ch, h], 0, PART)
            scale, inverse = scale_of(
                summed(ch, h, 0, [(second_in, near_scale(ch, h)), (third_in, third_scale)])
            )
            out_packed[y, ch, h] = pack(scale)

            def code(j, carry):
                out_codes[ch, 4 * y + j, part_rows[h]] = encode(sums[j], inverse)
                return carry

            lax.fori_loop(0, 4, code, 0)
            send_quarter(ch, h, 0, g2, 0)
            send_quarter(ch, h, 0, g, 1)

    def y_pass(ch):
        for h in range(2):
            g, g2 = gens[h]
            for copy in flying["q", ch, h, 0]:
                copy.wait()
            send_quarter(ch, h, g2, g, 2)

    def y_end(ch):
        for h in range(2):
            for n in (1, 2):
                for copy in flying["q", ch, h, n]:
                    copy.wait()

    def gram_block():
        mine = me % 20
        tall, wide = mine // 2, mine % 2
        from_ch = tall // 5
        at = pl.multiple_of(32 * (tall % 5), 32)

        def body(m, acc):
            for u in range(4):
                i = 4 * m + u
                a = s_split[from_ch, i, pl.ds(at, 32)]
                b = s_split[from_ch, i, pl.ds(HALF + at, 32)]
                c = s_split[wide, i, :HALF]
                d = s_split[wide, i, HALF:]
                acc = acc + (nt(a, c) + (nt(a, d) + nt(b, c)))
            return acc

        gram_parts[y] = lax.fori_loop(0, NB // 4, body, jnp.zeros((32, HALF), F32))
        ref = gram_parts.at[y]
        flying["y"] = [remote(ref, ref, sem_y.at[d], along_y(d)) for d in range(1, 4)]

    def gram_z():
        for copy in flying["y"]:
            copy.wait()
        gram_all[x, z, core] = (gram_parts[0] + gram_parts[1]) + (gram_parts[2] + gram_parts[3])
        ref = gram_all.at[x, z, core]
        flying["w0"] = [remote(ref, ref, sem_w.at[d], along_z(d)) for d in range(1, 4)]

    def gram_x():
        for copy in flying["w0"]:
            copy.wait()
        ref = gram_all.at[x, :, core]
        flying["w1"] = [remote(ref, ref, sem_w.at[3 + d], along_x(d)) for d in range(1, 4)]

    def gram_pair():
        for copy in flying["w1"]:
            copy.wait()
        ref = gram_all.at[:, :, core]
        flying["w2"] = [remote(ref, ref, sem_w.at[0], sibling)]

    def gram_whole():
        for copy in flying["w2"]:
            copy.wait()
        for tall in range(10):
            for wide in range(2):
                n = 2 * tall + wide
                work[32 * tall : 32 * tall + 32, HALF * wide : HALF * wide + HALF] = gram_all[
                    n // 8, n // 2 % 4, n % 2
                ] * (1.0 / ROWS)
        work[:, K:384] = jnp.zeros((K, 384 - K), F32)
        work[:, 384:] = (
            lax.broadcasted_iota(jnp.int32, (K, 384), 0) == lax.broadcasted_iota(jnp.int32, (K, 384), 1)
        ).astype(F32)

    def eliminate(b):
        top, bottom = b * BLK, b * BLK + BLK
        inverse = pivot_block(work[top:bottom, top:bottom])
        panel = nn(inverse, work[top:bottom, :], precision=HIGHEST)
        work[top:bottom, :] = panel
        if bottom < K:
            left = panel[:, bottom:K]
            lane = bottom // 128 * 128
            work[bottom:, lane:384] -= tn(left, panel[:, lane:384], precision=HIGHEST)
            edge = 384 + (bottom + 127) // 128 * 128
            work[bottom:, 384:edge] -= tn(left, panel[:, 384:edge], precision=HIGHEST)

    def leave():
        factor[...] = work[:, 384:]

    schedule = [
        (join, 0), (b_send, 0), (join, 1), (b_take, 0), (c_take, 0), (b_send, 1), (g1_take, 0), (b_take, 1),
        (g2_take, 0), (c_take, 1), (widen, 0), (g1_take, 1), (load_tiles.wait,), (project, 0), (y_send, 0),
        (g2_take, 1), (widen, 1), (y_third, 0), (project, 1), (y_send, 1),
        (gram_block,), (y_third, 1), (y_share, 0), (gram_z,), (gram_x,), (gram_pair,), (y_share, 1), (gram_whole,),
        (y_pass, 0), (eliminate, 0), (eliminate, 1), (y_pass, 1), (eliminate, 2), (eliminate, 3), (eliminate, 4),
        (leave,), (y_end, 0), (y_end, 1),
    ]
    for stage, *of in schedule:
        stage(*of)


def final_kernel(codes, packed, share, factor, projected_t, basis_t, left, right):
    step = pl.program_id(0)

    @pl.when(step == 0)
    def _():
        w = factor[:, :K]
        high, low = split(w)
        left[:, :K] = high
        left[:, K : 2 * K] = high
        left[:, 2 * K :] = low
        basis_t[...] = nn(w, share[...], precision=HIGHEST)

    for j in range(FCOLS):
        q = (step * FCOLS + j) // 4
        for ch in range(2):
            scale = jnp.concatenate([unpack(packed[q, ch, 0], 0, PART), unpack(packed[q, ch, 1], 0, PART)], axis=0)
            high, low = split(decode(codes[ch, j], scale))
            at = ch * HALF
            right[at : at + HALF] = high
            right[K + at : K + at + HALF] = low
            right[2 * K + at : 2 * K + at + HALF] = high
        projected_t[:, EDGE * j : EDGE * j + EDGE] = nn(left[...], right[...])


def whole(dims):
    return pl.BlockSpec(dims, lambda *_: (0,) * len(dims))


def vmem(n):
    return [pl.BlockSpec(memory_space=pltpu.VMEM)] * n


def smem(n):
    return [pl.BlockSpec(memory_space=pltpu.SMEM)] * n


def shape(dims, dtype):
    return jax.ShapeDtypeStruct(dims, dtype)


def local(tile_entries, slot_tile_row, slot_tile_column, tile_count, test_matrix):
    anywhere = pl.BlockSpec(memory_space=pl.ANY)
    params = pltpu.CompilerParams(vmem_limit_bytes=VMEM_LIMIT)
    dma = pltpu.SemaphoreType.DMA
    I32 = jnp.int32
    V = pltpu.VMEM

    codes, packed, order, order_row, start = pl.pallas_call(
        sample_kernel,
        in_specs=smem(3) + [anywhere, anywhere],
        out_specs=vmem(2) + smem(3),
        out_shape=[
            shape((2, NB, 2, HALF, 128), I16), shape((8, 128), F32),
            shape((SLOTS,), I32), shape((SLOTS,), I32), shape((NB + 1,), I32),
        ],
        scratch_shapes=[
            V((SLOTS, EDGE, EDGE), BF16), V((K, NB * EDGE), BF16), V((NB + 1, K, EDGE), F32),
            pltpu.SMEM((NB + 1,), I32), dma((GROUPS + 1,)),
        ],
        compiler_params=params,
        name="sample",
    )(slot_tile_row, slot_tile_column, tile_count, tile_entries, test_matrix.T)

    quarters = V((2, 2, 4, PART, EDGE), I16)
    share, out_codes, out_packed, factor = pl.pallas_call(
        main_kernel,
        in_specs=smem(3) + vmem(2) + [anywhere],
        out_specs=vmem(4),
        out_shape=[
            shape((K, 128), F32), shape((2, NB, HALF, EDGE), I16), shape((4, 2, 2, 8, 128), F32), shape((K, 384), F32),
        ],
        scratch_shapes=[
            V((2, NB, HALF, 128), I16), V((8, 128), F32), V((2, NB, HALF, 128), F32),
            V((2, 2, 3, 4, PART, 128), I16), V((2, 2, 3, 4, PART, 128), I16),
            V((2, 2, 3, PART, 128), I16), V((2, 2, 3, PART, 128), I16),
            V((2, 2, 8, 128), F32), V((2, 2, 3, 8, 128), F32),
            V((2, 2, 8, 128), F32), V((2, 2, 3, 8, 128), F32),
            V((2, 4, 4, 2, HALF, 128), I16), V((2, 4, 4, 2, 8, 128), F32),
            V((2, NB, K, EDGE), BF16), V((SLOTS, EDGE, EDGE), BF16), V((SLOTS + 1, HALF, EDGE), F32),
            V((2, NB, HALF, EDGE), I16), V((2, 8, 128), F32),
            quarters, quarters, quarters, quarters, V((4, PART, EDGE), F32),
            V((2, 2, 8, 128), F32), V((2, 2, 8, 128), F32), V((2, 2, 8, 128), F32),
            V((4, 32, HALF), F32), V((4, 4, 2, 32, HALF), F32), V((K, 768), F32),
            dma, dma((3, 2)), dma((2, 2, 6, 2)), dma((2, 2, 6, 2)),
            dma((2, 2, 4, 2)), dma((2, 2, 4, 2)), dma((2, 4, 2)), dma((2, 4, 2)), dma((2, 2)), dma((2, 2)),
            dma((2, 2, 2, 2)), dma((2, 2, 2)), dma((2, 2, 2)), dma((2, 2, 2)),
            dma((2, 2, 3, 2)), dma((2, 2, 3, 2)), dma((4, 2)), dma((7, 2)),
        ],
        compiler_params=pltpu.CompilerParams(
            vmem_limit_bytes=VMEM_LIMIT, collective_id=0, has_side_effects=True
        ),
        name="plane_and_ring_sums",
    )(order, order_row, start, codes, packed, tile_entries)

    projected_t, basis_t = pl.pallas_call(
        final_kernel,
        grid=(FSTEPS,),
        in_specs=[
            pl.BlockSpec((2, FCOLS, HALF, EDGE), lambda i: (0, i, 0, 0)),
            whole((4, 2, 2, 8, 128)), whole((K, 128)), whole((K, 384)),
        ],
        out_specs=[pl.BlockSpec((K, FCOLS * EDGE), lambda i: (0, i)), whole((K, 128))],
        out_shape=[shape((K, NB * EDGE), F32), shape((K, 128), F32)],
        scratch_shapes=[V((K, 3 * K), BF16), V((3 * K, EDGE), BF16)],
        compiler_params=params,
        name="final",
    )(out_codes, out_packed, share, factor)
    return (basis_t.T, projected_t.T)


def solution(mesh):
    placed = (
        P(("grp", "col"), None, None),
        P(("grp", "col")),
        P(("grp", "col")),
        P(("grp", "col")),
        P("col", None),
    )
    return jax.shard_map(
        local,
        mesh=mesh,
        in_specs=placed,
        out_specs=(P(("grp", "col"), None), P("col", None)),
        check_vma=False,
    )
```

```python
import functools

import jax
import jax.numpy as jnp
from jax import lax
from jax.experimental import pallas as pl
from jax.experimental.pallas import tpu as pltpu
from jax.sharding import PartitionSpec as P

MESH = pl.DeviceIdType.MESH
EDGE = 256
K = 320
HALF = 160
PART = 80
SLOTS = 72
GROUP = 24
GROUPS = SLOTS // GROUP
RUN = 24
NB = 16
BLK = 64
ROWS = 16384
FCOLS = 8
FSTEPS = NB // FCOLS
F32 = jnp.float32
BF16 = jnp.bfloat16
I16 = jnp.int16
VMEM_LIMIT = 60 * 1024 * 1024
HIGHEST = lax.Precision.HIGHEST


def nn(a, b, **kw):
    return lax.dot_general(a, b, (((1,), (0,)), ((), ())), preferred_element_type=F32, **kw)


def nt(a, b, **kw):
    return lax.dot_general(a, b, (((1,), (1,)), ((), ())), preferred_element_type=F32, **kw)


def tn(a, b, **kw):
    return lax.dot_general(a, b, (((0,), (0,)), ((), ())), preferred_element_type=F32, **kw)


def scale_of(peak):
    top = jnp.maximum(jnp.max(peak, axis=1, keepdims=True), 1e-30)
    return top * (1.0 / 32767.0), 32767.0 / top


def encode(value, inverse):
    return jnp.round(value * inverse).astype(jnp.int32).astype(I16)


def decode(code, scale):
    return code.astype(jnp.int32).astype(F32) * scale


def pack(scale, first=0):
    lane = lax.broadcasted_iota(jnp.int32, (8, 128), 1)
    packed = jnp.zeros((8, 128), F32)
    for m in range(scale.shape[0] // 8):
        packed = jnp.where(lane == first + m, scale[8 * m : 8 * m + 8], packed)
    return packed


def unpack(packed, first, rows):
    return jnp.concatenate([packed[:, first + m : first + m + 1] for m in range(rows // 8)], axis=0)


def split(value):
    high = value.astype(BF16)
    return high, (value - high.astype(F32)).astype(BF16)


def sample_kernel(
    row_s, col_s, count_s, tiles_hbm, omega_hbm,
    codes, packed, plan,
    tiles, omega, acc, fill, out, sems, sem_out,
):
    load_omega = pltpu.make_async_copy(omega_hbm, omega, sems.at[GROUPS])
    load_omega.start()
    loads = []
    for n in range(GROUPS):
        part = pl.ds(n * GROUP, GROUP)
        loads.append(pltpu.make_async_copy(tiles_hbm.at[part], tiles.at[part], sems.at[n]))
        loads[-1].start()

    def clear(i, carry):
        acc[i] = jnp.zeros((K, EDGE), F32)
        return carry

    lax.fori_loop(0, NB, clear, 0)

    def bin_of(slot):
        return jnp.where(slot < count_s[0], col_s[slot], NB)

    for c in range(NB + 1):
        fill[c] = 0

    def count(slot, carry):
        c = bin_of(slot)
        fill[c] = fill[c] + 1
        return carry

    lax.fori_loop(0, SLOTS, count, 0)
    begin = jnp.int32(0)
    for c in range(NB + 1):
        plan[2 * SLOTS + c] = begin
        size = fill[c]
        fill[c] = begin
        begin = begin + size

    def put(slot, carry):
        c = bin_of(slot)
        at = fill[c]
        fill[c] = at + 1
        plan[at] = slot
        plan[SLOTS + at] = row_s[slot]
        return carry

    lax.fori_loop(0, SLOTS, put, 0)

    load_omega.wait()
    for n in range(GROUPS):
        loads[n].wait()
        for u in range(GROUP):
            slot = n * GROUP + u
            row = jnp.where(slot < count_s[0], row_s[slot], NB)
            left = omega[:, pl.ds(pl.multiple_of(col_s[slot] * EDGE, EDGE), EDGE)]
            acc[row] += nt(left, tiles[slot])

    def peak_step(i, peak):
        block = jnp.abs(acc[i])
        return jnp.maximum(peak, jnp.maximum(block[:, :128], block[:, 128:]))

    scale, inverse = scale_of(lax.fori_loop(0, NB, peak_step, jnp.zeros((K, 128), F32)))
    packed[...] = pack(scale)

    def code_step(i, carry):
        code = encode(acc[i], inverse)
        for ch in range(2):
            for core in range(2):
                out[i, ch, core] = code[ch * HALF : ch * HALF + HALF, core * 128 : core * 128 + 128]
        pltpu.make_async_copy(out.at[i, 0], codes.at[0, i], sem_out.at[0, i]).start()
        pltpu.make_async_copy(out.at[i, 1], codes.at[1, i], sem_out.at[1, i]).start()
        return carry

    lax.fori_loop(0, NB, code_step, 0)

    def out_step(i, carry):
        pltpu.make_async_copy(out.at[i, 0], codes.at[0, i], sem_out.at[0, i]).wait()
        pltpu.make_async_copy(out.at[i, 1], codes.at[1, i], sem_out.at[1, i]).wait()
        return carry

    lax.fori_loop(0, NB, out_step, 0)


def xor2(a, b):
    return (a % 2 + b % 2) % 2 + 2 * ((a // 2 + b // 2) % 2)


def pivot_block(block):
    n = BLK // 8
    eye = (
        lax.broadcasted_iota(jnp.int32, (BLK, BLK), 0) == lax.broadcasted_iota(jnp.int32, (BLK, BLK), 1)
    ).astype(F32)
    whole = jnp.concatenate([block, eye], axis=1)
    parts = [whole[8 * g : 8 * g + 8] for g in range(n)]
    sub = lax.broadcasted_iota(jnp.int32, (8, 128), 0)
    for k in range(0, BLK, 4):
        home, at = k // 8, k % 8
        cols = [
            [jnp.broadcast_to(parts[g][:, k + i : k + i + 1], (8, 128)) for g in range(home, n)] for i in range(4)
        ]
        rows = [parts[home][at + i : at + i + 1] for i in range(4)]
        steps = []
        roots = []
        for i in range(4):
            pivot = cols[i][0][at + i : at + i + 1]
            inverse = 1.0 / pivot
            roots.append(lax.rsqrt(pivot))
            steps.append(rows[i] * inverse)
            for j in range(i + 1, 4):
                rows[j] = rows[j] - cols[i][0][at + j : at + j + 1] * steps[i]
                factor = cols[j][0][at + i : at + i + 1] * inverse
                cols[j] = [c - b * factor for c, b in zip(cols[j], cols[i])]
        for g in range(home, n):
            new = parts[g]
            for i in range(4):
                new = new - cols[i][g - home] * steps[i]
            if g == home:
                new = jnp.where(sub > at + 3, new, parts[g])
                for i in range(4):
                    new = jnp.where(sub == at + i, rows[i] * roots[i], new)
            parts[g] = new
    return jnp.concatenate(parts, axis=0)[:, BLK:]

def main_kernel(
    plan, codes, packed, tiles_hbm,
    share, result, out_packed, factor,
    out_codes, own_codes, pair_codes, pair_packed, total, sb, rb, sc, rc, sbp, rbp, scp, rcp, gat, gat_packed,
    s_split, tiles, prefix, p_codes, p_packed,
    first_in, second_in, third_in, third_out, sums, near_packed, third_packed_in, third_packed_out,
    gram_parts, gram_all, work,
    sem_t, sem_own, sem_pair, sem_b, sem_c, sem_g1, sem_g2, sem_gp1, sem_gp2, sem_f, sem_fp,
    sem_a, sem_p, sem_3, sem_3p, sem_g, sem_gp, sem_y, sem_w, sem_out,
):
    y = lax.axis_index("grp")
    me = lax.axis_index("col")
    chip, core = me // 2, me % 2
    x, z = chip // 4, chip % 4
    other = 1 - core
    sibling = {"col": chip * 2 + other}

    def along_x(d):
        return {"col": (xor2(x, d) * 4 + z) * 2 + core}

    def along_z(d):
        return {"col": (x * 4 + xor2(z, d)) * 2 + core}

    def along_y(d):
        return {"grp": xor2(y, d)}

    load_tiles = pltpu.make_async_copy(tiles_hbm, tiles, sem_t)

    barrier = pltpu.get_barrier_semaphore()
    greeted = [sibling] + [f(d) for f in (along_x, along_z, along_y) for d in (1, 2, 3)]
    for peer in greeted:
        pl.semaphore_signal(barrier, inc=1, device_id=peer, device_id_type=MESH)
    pl.semaphore_wait(barrier, len(greeted))

    def remote(src, dst, sems, peer):
        copy = pltpu.make_async_remote_copy(
            src_ref=src, dst_ref=dst, send_sem=sems.at[0], recv_sem=sems.at[1],
            device_id=peer, device_id_type=MESH,
        )
        copy.start()
        return copy

    pair = {
        ch: remote(codes.at[ch, :, other], pair_codes.at[ch], sem_pair.at[ch], sibling) for ch in range(2)
    }
    own = {ch: pltpu.make_async_copy(codes.at[ch, :, core], own_codes.at[ch], sem_own.at[ch]) for ch in range(2)}
    for ch in range(2):
        own[ch].start()
    pair_scales = remote(packed, pair_packed, sem_pair.at[2], sibling)
    pair_scales.wait()

    def join(ch):
        own[ch].wait()
        pair[ch].wait()
        own_scale = unpack(packed[...], 20 * ch, HALF)
        pair_scale = unpack(pair_packed[...], 20 * ch, HALF)

        def body(w, carry):
            i = xor2(x, w // 4) * 4 + xor2(z, w % 4)
            total[ch, w] = decode(own_codes[ch, i], own_scale) + decode(pair_codes[ch, i], pair_scale)
            return carry

        lax.fori_loop(0, NB, body, 0)

    def block(p, a, b):
        return 4 * a + b if p == 0 else 4 * b + a

    outer = (along_x, along_z)
    inner = (along_z, along_x)
    part_rows = [slice(p * PART, p * PART + PART) for p in range(2)]
    part_at = [pl.ds(p * PART, PART) for p in range(2)]
    flying = {}

    def b_send(ch):
        for p in range(2):
            peak = jnp.zeros((PART, 128), F32)
            for d in range(1, 4):
                for e in range(4):
                    peak = jnp.maximum(peak, jnp.abs(total[ch, block(p, d, e), part_rows[p]]))
            scale, inverse = scale_of(peak)
            sbp[ch, p] = pack(scale)
            flying["b", ch, p] = []
            for d in range(1, 4):
                for e in range(4):
                    sb[ch, p, d - 1, e] = encode(total[ch, block(p, d, e), part_rows[p]], inverse)
                flying["b", ch, p] += [
                    remote(sb.at[ch, p, d - 1], rb.at[ch, p, d - 1], sem_b.at[ch, p, d - 1], outer[p](d)),
                    remote(sbp.at[ch, p], rbp.at[ch, p, d - 1], sem_b.at[ch, p, d + 2], outer[p](d)),
                ]

    def b_take(ch):
        for p in range(2):
            for copy in flying["b", ch, p]:
                copy.wait()
            scales = [unpack(rbp[ch, p, d], 0, PART) for d in range(3)]
            peak = jnp.zeros((PART, 128), F32)
            for e in range(4):
                at = block(p, 0, e)
                value = total[ch, at, part_rows[p]]
                for d in range(3):
                    value = value + decode(rb[ch, p, d, e], scales[d])
                total[ch, at, part_rows[p]] = value
                if e > 0:
                    peak = jnp.maximum(peak, jnp.abs(value))
            scale, inverse = scale_of(peak)
            scp[ch, p] = pack(scale)
            flying["c", ch, p] = []
            for e in range(1, 4):
                sc[ch, p, e - 1] = encode(total[ch, block(p, 0, e), part_rows[p]], inverse)
                flying["c", ch, p] += [
                    remote(sc.at[ch, p, e - 1], rc.at[ch, p, e - 1], sem_c.at[ch, p, e - 1], inner[p](e)),
                    remote(scp.at[ch, p], rcp.at[ch, p, e - 1], sem_c.at[ch, p, e + 2], inner[p](e)),
                ]

    def c_take(ch):
        for p in range(2):
            for copy in flying["c", ch, p]:
                copy.wait()
            value = total[ch, 0, part_rows[p]]
            for e in range(3):
                value = value + decode(rc[ch, p, e], unpack(rcp[ch, p, e], 0, PART))
            share[ch * HALF + p * PART : ch * HALF + p * PART + PART, :] = value
        mine = share[ch * HALF : ch * HALF + HALF, :]
        scale, inverse = scale_of(jnp.abs(mine))
        gat[ch, x, z, core] = encode(mine, inverse)
        gat_packed[ch, x, z, core] = pack(scale)
        flying["g1", ch] = []
        for d in range(1, 4):
            for p in range(2):
                ref = gat.at[ch, x, z, core, part_at[p]]
                flying["g1", ch].append(remote(ref, ref, sem_g1.at[ch, p, d], inner[p](d)))
            ref = gat_packed.at[ch, x, z, core]
            flying["g1", ch].append(remote(ref, ref, sem_gp1.at[ch, d], inner[0](d)))

    def g1_take(ch):
        for copy in flying["g1", ch]:
            copy.wait()
        flying["g2", ch] = []
        for d in range(1, 4):
            ref = gat.at[ch, x, :, core, part_at[0]]
            flying["g2", ch].append(remote(ref, ref, sem_g2.at[ch, 0, d], along_x(d)))
            ref = gat.at[ch, :, z, core, part_at[1]]
            flying["g2", ch].append(remote(ref, ref, sem_g2.at[ch, 1, d], along_z(d)))
            ref = gat_packed.at[ch, x, :, core]
            flying["g2", ch].append(remote(ref, ref, sem_gp2.at[ch, d], along_x(d)))

    def g2_take(ch):
        for copy in flying["g2", ch]:
            copy.wait()
        ref, packed_ref = gat.at[ch, :, :, core], gat_packed.at[ch, :, :, core]
        flying["f", ch] = [
            remote(ref, ref, sem_f.at[ch], sibling),
            remote(packed_ref, packed_ref, sem_fp.at[ch], sibling),
        ]

    def widen(ch):
        for copy in flying["f", ch]:
            copy.wait()

        def body(i, carry):
            for c in range(2):
                lanes = slice(c * 128, c * 128 + 128)
                scale = unpack(gat_packed[ch, i // 4, i % 4, c], 0, HALF)
                high, low = split(decode(gat[ch, i // 4, i % 4, c], scale))
                s_split[ch, i, :HALF, lanes] = high
                s_split[ch, i, HALF:, lanes] = low
            return carry

        lax.fori_loop(0, NB, body, 0)

    def project(ch):
        prefix[0] = jnp.zeros((HALF, EDGE), F32)

        def body(m, carry):
            for u in range(RUN):
                n = m * RUN + u
                both = nn(s_split[ch, plan[SLOTS + n]], tiles[plan[n]])
                prefix[n + 1] = prefix[n] + (both[:HALF] + both[HALF:])
            return carry

        lax.fori_loop(0, SLOTS // RUN, body, 0)

        def value_of(j):
            return prefix[plan[2 * SLOTS + j + 1]] - prefix[plan[2 * SLOTS + j]]

        def peak_step(j, peak):
            value = jnp.abs(value_of(j))
            return jnp.maximum(peak, jnp.maximum(value[:, :128], value[:, 128:]))

        scale, inverse = scale_of(lax.fori_loop(0, NB, peak_step, jnp.zeros((HALF, 128), F32)))
        p_packed[ch] = pack(scale)

        def code_step(j, carry):
            p_codes[ch, j] = encode(value_of(j), inverse)
            return carry

        lax.fori_loop(0, NB, code_step, 0)

    gens = ((1, 3), (3, 1))
    line = {1: 0, 3: 1}

    def quarter(w):
        return pl.ds(pl.multiple_of(4 * xor2(y, w), 4), 4)

    def y_start(ch, n):
        for h in range(2):
            g, g2 = gens[h]
            w, target = ((2, first_in), (g, second_in))[n]
            flying["a", ch, h, n] = remote(
                p_codes.at[ch, quarter(w), part_at[h]], target.at[ch, h], sem_a.at[ch, h, n], along_y(g)
            )

    def y_first(ch):
        flying["p", ch] = [
            remote(p_packed.at[ch], near_packed.at[ch, n], sem_p.at[ch, n], along_y(g)) for n, g in enumerate((1, 3))
        ]
        y_start(ch, 0)

    def y_second(ch):
        y_start(ch, 1)

    def summed(ch, h, w, takes):
        at = 4 * xor2(y, w)
        own_scale = unpack(p_packed[ch], 10 * h, PART)

        def body(j, peak):
            value = decode(p_codes[ch, at + j, part_rows[h]], own_scale)
            for ref, scale in takes:
                value = value + decode(ref[ch, h, j], scale)
            sums[j] = value
            value = jnp.abs(value)
            return jnp.maximum(peak, jnp.maximum(value[:, :128], value[:, 128:]))

        return lax.fori_loop(0, 4, body, jnp.zeros((PART, 128), F32))

    def near_scale(ch, h):
        return unpack(near_packed[ch, line[gens[h][0]]], 10 * h, PART)

    def y_third(ch):
        for copy in flying["p", ch]:
            copy.wait()
        for h in range(2):
            g, g2 = gens[h]
            flying["a", ch, h, 0].wait()
            scale, inverse = scale_of(summed(ch, h, g2, [(first_in, near_scale(ch, h))]))
            third_packed_out[ch, h] = pack(scale)

            def code(j, carry):
                third_out[ch, h, j] = encode(sums[j], inverse)
                return carry

            lax.fori_loop(0, 4, code, 0)
            flying["3", ch, h] = [
                remote(third_packed_out.at[ch, h], third_packed_in.at[ch, h], sem_3p.at[ch, h], along_y(g2)),
                remote(third_out.at[ch, h], third_in.at[ch, h], sem_3.at[ch, h], along_y(g2)),
            ]

    def send_quarter(ch, h, w, g, n):
        ref = out_codes.at[ch, quarter(w), part_at[h]]
        packed_ref = out_packed.at[xor2(y, w), ch, h]
        flying["q", ch, h, n] = [
            remote(ref, ref, sem_g.at[ch, h, n], along_y(g)),
            remote(packed_ref, packed_ref, sem_gp.at[ch, h, n], along_y(g)),
        ]

    written = []

    def write(ch, h, w):
        at = (ch, quarter(w), part_at[h])
        written.append(pltpu.make_async_copy(out_codes.at[at], result.at[at], sem_out.at[ch, h, w]))
        written[-1].start()

    def y_share(ch):
        for h in range(2):
            g, g2 = gens[h]
            flying["a", ch, h, 1].wait()
            for copy in flying["3", ch, h]:
                copy.wait()
            third_scale = unpack(third_packed_in[ch, h], 0, PART)
            scale, inverse = scale_of(
                summed(ch, h, 0, [(second_in, near_scale(ch, h)), (third_in, third_scale)])
            )
            out_packed[y, ch, h] = pack(scale)

            def code(j, carry):
                out_codes[ch, 4 * y + j, part_rows[h]] = encode(sums[j], inverse)
                return carry

            lax.fori_loop(0, 4, code, 0)
            send_quarter(ch, h, 0, g2, 0)
            send_quarter(ch, h, 0, g, 1)
            write(ch, h, 0)

    def y_pass(ch):
        for h in range(2):
            g, g2 = gens[h]
            for copy in flying["q", ch, h, 0]:
                copy.wait()
            send_quarter(ch, h, g2, g, 2)
            write(ch, h, g2)

    def y_end(ch):
        for h in range(2):
            for n, w in ((1, gens[h][0]), (2, 2)):
                for copy in flying["q", ch, h, n]:
                    copy.wait()
                write(ch, h, w)

    def gram_block():
        mine = me % 20
        tall, wide = mine // 2, mine % 2
        from_ch = tall // 5
        at = pl.multiple_of(32 * (tall % 5), 32)

        def body(m, acc):
            for u in range(4):
                i = 4 * m + u
                a = s_split[from_ch, i, pl.ds(at, 32)]
                b = s_split[from_ch, i, pl.ds(HALF + at, 32)]
                c = s_split[wide, i, :HALF]
                d = s_split[wide, i, HALF:]
                acc = acc + (nt(a, c) + (nt(a, d) + nt(b, c)))
            return acc

        gram_parts[y] = lax.fori_loop(0, NB // 4, body, jnp.zeros((32, HALF), F32))
        ref = gram_parts.at[y]
        flying["y"] = [remote(ref, ref, sem_y.at[d], along_y(d)) for d in range(1, 4)]

    def gram_z():
        for copy in flying["y"]:
            copy.wait()
        gram_all[x, z, core] = (gram_parts[0] + gram_parts[1]) + (gram_parts[2] + gram_parts[3])
        ref = gram_all.at[x, z, core]
        flying["w0"] = [remote(ref, ref, sem_w.at[d], along_z(d)) for d in range(1, 4)]

    def gram_x():
        for copy in flying["w0"]:
            copy.wait()
        ref = gram_all.at[x, :, core]
        flying["w1"] = [remote(ref, ref, sem_w.at[3 + d], along_x(d)) for d in range(1, 4)]

    def gram_pair():
        for copy in flying["w1"]:
            copy.wait()
        ref = gram_all.at[:, :, core]
        flying["w2"] = [remote(ref, ref, sem_w.at[0], sibling)]

    def gram_whole():
        for copy in flying["w2"]:
            copy.wait()
        for tall in range(10):
            for wide in range(2):
                n = 2 * tall + wide
                work[32 * tall : 32 * tall + 32, HALF * wide : HALF * wide + HALF] = gram_all[
                    n // 8, n // 2 % 4, n % 2
                ] * (1.0 / ROWS)
        work[:, K:384] = jnp.zeros((K, 384 - K), F32)
        work[:, 384:] = (
            lax.broadcasted_iota(jnp.int32, (K, 384), 0) == lax.broadcasted_iota(jnp.int32, (K, 384), 1)
        ).astype(F32)

    def eliminate(b):
        top, bottom = b * BLK, b * BLK + BLK
        inverse = pivot_block(work[top:bottom, top:bottom])
        panel = nn(inverse, work[top:bottom, :], precision=HIGHEST)
        work[top:bottom, :] = panel
        if bottom < K:
            left = panel[:, bottom:K]
            lane = bottom // 128 * 128
            work[bottom:, lane:384] -= tn(left, panel[:, lane:384], precision=HIGHEST)
            edge = 384 + (bottom + 127) // 128 * 128
            work[bottom:, 384:edge] -= tn(left, panel[:, 384:edge], precision=HIGHEST)

    def leave():
        factor[...] = work[:, 384:]

    schedule = [
        (join, 0), (b_send, 0), (join, 1), (load_tiles.start,), (b_take, 0), (c_take, 0), (b_send, 1), (g1_take, 0), (b_take, 1),
        (g2_take, 0), (c_take, 1), (widen, 0), (g1_take, 1), (load_tiles.wait,), (project, 0), (y_first, 0), (y_second, 0),
        (g2_take, 1), (widen, 1), (project, 1), (y_first, 1), (y_third, 0), (gram_block,), (y_second, 1),
        (y_third, 1), (y_share, 0), (gram_z,), (gram_x,), (gram_pair,), (y_share, 1), (gram_whole,),
        (y_pass, 0), (eliminate, 0), (eliminate, 1), (y_pass, 1), (eliminate, 2), (eliminate, 3), (eliminate, 4),
        (leave,), (y_end, 0), (y_end, 1),
    ]
    for stage, *of in schedule:
        stage(*of)
    for copy in written:
        copy.wait()


def final_kernel(codes, packed, share, factor, projected_t, basis_t, left, right):
    step = pl.program_id(0)

    @pl.when(step == 0)
    def _():
        w = factor[:, :K]
        high, low = split(w)
        left[:, :K] = high
        left[:, K : 2 * K] = high
        left[:, 2 * K :] = low
        basis_t[...] = nn(w, share[...], precision=HIGHEST)

    for j in range(FCOLS):
        q = (step * FCOLS + j) // 4
        for ch in range(2):
            scale = jnp.concatenate([unpack(packed[q, ch, 0], 0, PART), unpack(packed[q, ch, 1], 0, PART)], axis=0)
            high, low = split(decode(codes[ch, j], scale))
            at = ch * HALF
            right[at : at + HALF] = high
            right[K + at : K + at + HALF] = low
            right[2 * K + at : 2 * K + at + HALF] = high
        projected_t[:, EDGE * j : EDGE * j + EDGE] = nn(left[...], right[...])


def whole(dims):
    return pl.BlockSpec(dims, lambda *_: (0,) * len(dims))


def vmem(n):
    return [pl.BlockSpec(memory_space=pltpu.VMEM)] * n


def smem(n):
    return [pl.BlockSpec(memory_space=pltpu.SMEM)] * n


def shape(dims, dtype):
    return jax.ShapeDtypeStruct(dims, dtype)


def local(tile_entries, slot_tile_row, slot_tile_column, tile_count, test_matrix):
    anywhere = pl.BlockSpec(memory_space=pl.ANY)
    params = pltpu.CompilerParams(vmem_limit_bytes=VMEM_LIMIT)
    dma = pltpu.SemaphoreType.DMA
    I32 = jnp.int32
    V = pltpu.VMEM

    codes, packed, plan = pl.pallas_call(
        sample_kernel,
        in_specs=smem(3) + [anywhere, anywhere],
        out_specs=[anywhere] + vmem(1) + smem(1),
        out_shape=[
            shape((2, NB, 2, HALF, 128), I16), shape((8, 128), F32),
            shape((2 * SLOTS + NB + 1,), I32),
        ],
        scratch_shapes=[
            V((SLOTS, EDGE, EDGE), BF16), V((K, NB * EDGE), BF16), V((NB + 1, K, EDGE), F32),
            pltpu.SMEM((NB + 1,), I32), V((NB, 2, 2, HALF, 128), I16), dma((GROUPS + 1,)), dma((2, NB)),
        ],
        compiler_params=params,
        name="sample",
    )(slot_tile_row, slot_tile_column, tile_count, tile_entries, test_matrix.T)

    quarters = V((2, 2, 4, PART, EDGE), I16)
    share, out_codes, out_packed, factor = pl.pallas_call(
        main_kernel,
        in_specs=smem(1) + [anywhere] + vmem(1) + [anywhere],
        out_specs=vmem(1) + [anywhere] + vmem(2),
        out_shape=[
            shape((K, 128), F32), shape((2, NB, HALF, EDGE), I16), shape((4, 2, 2, 8, 128), F32), shape((K, 384), F32),
        ],
        scratch_shapes=[
            V((2, NB, HALF, EDGE), I16), V((2, NB, HALF, 128), I16), V((2, NB, HALF, 128), I16), V((8, 128), F32), V((2, NB, HALF, 128), F32),
            V((2, 2, 3, 4, PART, 128), I16), V((2, 2, 3, 4, PART, 128), I16),
            V((2, 2, 3, PART, 128), I16), V((2, 2, 3, PART, 128), I16),
            V((2, 2, 8, 128), F32), V((2, 2, 3, 8, 128), F32),
            V((2, 2, 8, 128), F32), V((2, 2, 3, 8, 128), F32),
            V((2, 4, 4, 2, HALF, 128), I16), V((2, 4, 4, 2, 8, 128), F32),
            V((2, NB, K, EDGE), BF16), V((SLOTS, EDGE, EDGE), BF16), V((SLOTS + 1, HALF, EDGE), F32),
            V((2, NB, HALF, EDGE), I16), V((2, 8, 128), F32),
            quarters, quarters, quarters, quarters, V((4, PART, EDGE), F32),
            V((2, 2, 8, 128), F32), V((2, 2, 8, 128), F32), V((2, 2, 8, 128), F32),
            V((4, 32, HALF), F32), V((4, 4, 2, 32, HALF), F32), V((K, 768), F32),
            dma, dma((2,)), dma((3, 2)), dma((2, 2, 6, 2)), dma((2, 2, 6, 2)),
            dma((2, 2, 4, 2)), dma((2, 2, 4, 2)), dma((2, 4, 2)), dma((2, 4, 2)), dma((2, 2)), dma((2, 2)),
            dma((2, 2, 2, 2)), dma((2, 2, 2)), dma((2, 2, 2)), dma((2, 2, 2)),
            dma((2, 2, 3, 2)), dma((2, 2, 3, 2)), dma((4, 2)), dma((7, 2)), dma((2, 2, 4)),
        ],
        compiler_params=pltpu.CompilerParams(
            vmem_limit_bytes=VMEM_LIMIT, collective_id=0, has_side_effects=True
        ),
        name="plane_and_ring_sums",
    )(plan, codes, packed, tile_entries)

    projected_t, basis_t = pl.pallas_call(
        final_kernel,
        grid=(FSTEPS,),
        in_specs=[
            pl.BlockSpec((2, FCOLS, HALF, EDGE), lambda i: (0, i, 0, 0)),
            whole((4, 2, 2, 8, 128)), whole((K, 128)), whole((K, 384)),
        ],
        out_specs=[pl.BlockSpec((K, FCOLS * EDGE), lambda i: (0, i)), whole((K, 128))],
        out_shape=[shape((K, NB * EDGE), F32), shape((K, 128), F32)],
        scratch_shapes=[V((K, 3 * K), BF16), V((3 * K, EDGE), BF16)],
        compiler_params=params,
        name="final",
    )(out_codes, out_packed, share, factor)
    return (basis_t.T, projected_t.T)


def solution(mesh):
    placed = (
        P(("grp", "col"), None, None),
        P(("grp", "col")),
        P(("grp", "col")),
        P(("grp", "col")),
        P("col", None),
    )
    return jax.shard_map(
        local,
        mesh=mesh,
        in_specs=placed,
        out_specs=(P(("grp", "col"), None), P("col", None)),
        check_vma=False,
    )
```

```python
import functools

import jax
import jax.numpy as jnp
from jax import lax
from jax.experimental import pallas as pl
from jax.experimental.pallas import tpu as pltpu
from jax.sharding import PartitionSpec as P

MESH = pl.DeviceIdType.MESH
EDGE = 256
K = 320
HALF = 160
PART = 80
SLOTS = 72
GROUP = 24
GROUPS = SLOTS // GROUP
RUN = 24
NB = 16
BLK = 64
ROWS = 16384
FCOLS = 8
FSTEPS = NB // FCOLS
F32 = jnp.float32
BF16 = jnp.bfloat16
I16 = jnp.int16
VMEM_LIMIT = 60 * 1024 * 1024
HIGHEST = lax.Precision.HIGHEST


def nn(a, b, **kw):
    return lax.dot_general(a, b, (((1,), (0,)), ((), ())), preferred_element_type=F32, **kw)


def nt(a, b, **kw):
    return lax.dot_general(a, b, (((1,), (1,)), ((), ())), preferred_element_type=F32, **kw)


def tn(a, b, **kw):
    return lax.dot_general(a, b, (((0,), (0,)), ((), ())), preferred_element_type=F32, **kw)


def scale_of(peak):
    top = jnp.maximum(jnp.max(peak, axis=1, keepdims=True), 1e-30)
    return top * (1.0 / 32767.0), 32767.0 / top


def encode(value, inverse):
    return jnp.round(value * inverse).astype(jnp.int32).astype(I16)


def decode(code, scale):
    return code.astype(jnp.int32).astype(F32) * scale


def pack(scale, first=0):
    lane = lax.broadcasted_iota(jnp.int32, (8, 128), 1)
    packed = jnp.zeros((8, 128), F32)
    for m in range(scale.shape[0] // 8):
        packed = jnp.where(lane == first + m, scale[8 * m : 8 * m + 8], packed)
    return packed


def unpack(packed, first, rows):
    return jnp.concatenate([packed[:, first + m : first + m + 1] for m in range(rows // 8)], axis=0)


def split(value):
    high = value.astype(BF16)
    return high, (value - high.astype(F32)).astype(BF16)


def sample_kernel(
    row_s, col_s, count_s, tiles_hbm, omega_hbm,
    codes, packed, plan,
    tiles, omega, acc, fill, out, sems, sem_out,
):
    load_omega = pltpu.make_async_copy(omega_hbm, omega, sems.at[GROUPS])
    load_omega.start()
    loads = []
    for n in range(GROUPS):
        part = pl.ds(n * GROUP, GROUP)
        loads.append(pltpu.make_async_copy(tiles_hbm.at[part], tiles.at[part], sems.at[n]))
        loads[-1].start()

    def clear(i, carry):
        acc[i] = jnp.zeros((K, EDGE), F32)
        return carry

    lax.fori_loop(0, NB, clear, 0)

    def bin_of(slot):
        return jnp.where(slot < count_s[0], col_s[slot], NB)

    for c in range(NB + 1):
        fill[c] = 0

    def count(slot, carry):
        c = bin_of(slot)
        fill[c] = fill[c] + 1
        return carry

    lax.fori_loop(0, SLOTS, count, 0)
    begin = jnp.int32(0)
    for c in range(NB + 1):
        plan[2 * SLOTS + c] = begin
        size = fill[c]
        fill[c] = begin
        begin = begin + size

    def put(slot, carry):
        c = bin_of(slot)
        at = fill[c]
        fill[c] = at + 1
        plan[at] = slot
        plan[SLOTS + at] = row_s[slot]
        return carry

    lax.fori_loop(0, SLOTS, put, 0)

    load_omega.wait()
    for n in range(GROUPS):
        loads[n].wait()
        for u in range(GROUP):
            slot = n * GROUP + u
            row = jnp.where(slot < count_s[0], row_s[slot], NB)
            left = omega[:, pl.ds(pl.multiple_of(col_s[slot] * EDGE, EDGE), EDGE)]
            acc[row] += nt(left, tiles[slot])

    def peak_step(i, peak):
        block = jnp.abs(acc[i])
        return jnp.maximum(peak, jnp.maximum(block[:, :128], block[:, 128:]))

    scale, inverse = scale_of(lax.fori_loop(0, NB, peak_step, jnp.zeros((K, 128), F32)))
    packed[...] = pack(scale)

    def code_step(i, carry):
        code = encode(acc[i], inverse)
        for ch in range(2):
            for core in range(2):
                out[i, ch, core] = code[ch * HALF : ch * HALF + HALF, core * 128 : core * 128 + 128]
        pltpu.make_async_copy(out.at[i, 0], codes.at[0, i], sem_out.at[0, i]).start()
        pltpu.make_async_copy(out.at[i, 1], codes.at[1, i], sem_out.at[1, i]).start()
        return carry

    lax.fori_loop(0, NB, code_step, 0)

    def out_step(i, carry):
        pltpu.make_async_copy(out.at[i, 0], codes.at[0, i], sem_out.at[0, i]).wait()
        pltpu.make_async_copy(out.at[i, 1], codes.at[1, i], sem_out.at[1, i]).wait()
        return carry

    lax.fori_loop(0, NB, out_step, 0)


def xor2(a, b):
    return (a % 2 + b % 2) % 2 + 2 * ((a // 2 + b // 2) % 2)


def pivot_block(block):
    n = BLK // 8
    eye = (
        lax.broadcasted_iota(jnp.int32, (BLK, BLK), 0) == lax.broadcasted_iota(jnp.int32, (BLK, BLK), 1)
    ).astype(F32)
    whole = jnp.concatenate([block, eye], axis=1)
    parts = [whole[8 * g : 8 * g + 8] for g in range(n)]
    sub = lax.broadcasted_iota(jnp.int32, (8, 128), 0)
    for k in range(0, BLK, 4):
        home, at = k // 8, k % 8
        cols = [
            [jnp.broadcast_to(parts[g][:, k + i : k + i + 1], (8, 128)) for g in range(home, n)] for i in range(4)
        ]
        rows = [parts[home][at + i : at + i + 1] for i in range(4)]
        steps = []
        roots = []
        for i in range(4):
            pivot = cols[i][0][at + i : at + i + 1]
            inverse = 1.0 / pivot
            roots.append(lax.rsqrt(pivot))
            steps.append(rows[i] * inverse)
            for j in range(i + 1, 4):
                rows[j] = rows[j] - cols[i][0][at + j : at + j + 1] * steps[i]
                factor = cols[j][0][at + i : at + i + 1] * inverse
                cols[j] = [c - b * factor for c, b in zip(cols[j], cols[i])]
        for g in range(home, n):
            new = parts[g]
            for i in range(4):
                new = new - cols[i][g - home] * steps[i]
            if g == home:
                new = jnp.where(sub > at + 3, new, parts[g])
                for i in range(4):
                    new = jnp.where(sub == at + i, rows[i] * roots[i], new)
            parts[g] = new
    return jnp.concatenate(parts, axis=0)[:, BLK:]

def main_kernel(
    plan, codes, packed, tiles_hbm,
    share, result, out_packed, factor,
    out_codes, own_codes, pair_codes, pair_packed, total, sb, rb, sc, rc, sbp, rbp, scp, rcp, gat, gat_packed,
    s_split, tiles, prefix, p_codes, p_packed,
    first_in, second_in, third_in, third_out, sums, near_packed, third_packed_in, third_packed_out,
    gram_parts, gram_all, work,
    sem_t, sem_own, sem_pair, sem_b, sem_c, sem_g1, sem_g2, sem_gp1, sem_gp2, sem_f, sem_fp,
    sem_a, sem_p, sem_3, sem_3p, sem_g, sem_gp, sem_y, sem_w, sem_out,
):
    y = lax.axis_index("grp")
    me = lax.axis_index("col")
    chip, core = me // 2, me % 2
    x, z = chip // 4, chip % 4
    other = 1 - core
    sibling = {"col": chip * 2 + other}

    def along_x(d):
        return {"col": (xor2(x, d) * 4 + z) * 2 + core}

    def along_z(d):
        return {"col": (x * 4 + xor2(z, d)) * 2 + core}

    def along_y(d):
        return {"grp": xor2(y, d)}

    load_tiles = pltpu.make_async_copy(tiles_hbm, tiles, sem_t)

    barrier = pltpu.get_barrier_semaphore()
    greeted = [sibling] + [f(d) for f in (along_x, along_z, along_y) for d in (1, 2, 3)]
    for peer in greeted:
        pl.semaphore_signal(barrier, inc=1, device_id=peer, device_id_type=MESH)
    pl.semaphore_wait(barrier, len(greeted))

    def remote(src, dst, sems, peer):
        copy = pltpu.make_async_remote_copy(
            src_ref=src, dst_ref=dst, send_sem=sems.at[0], recv_sem=sems.at[1],
            device_id=peer, device_id_type=MESH,
        )
        copy.start()
        return copy

    pair = {
        ch: remote(codes.at[ch, :, other], pair_codes.at[ch], sem_pair.at[ch], sibling) for ch in range(2)
    }
    own = {ch: pltpu.make_async_copy(codes.at[ch, :, core], own_codes.at[ch], sem_own.at[ch]) for ch in range(2)}
    for ch in range(2):
        own[ch].start()
    pair_scales = remote(packed, pair_packed, sem_pair.at[2], sibling)
    pair_scales.wait()

    def join(ch):
        own[ch].wait()
        pair[ch].wait()
        own_scale = unpack(packed[...], 20 * ch, HALF)
        pair_scale = unpack(pair_packed[...], 20 * ch, HALF)

        def body(w, carry):
            i = xor2(x, w // 4) * 4 + xor2(z, w % 4)
            total[ch, w] = decode(own_codes[ch, i], own_scale) + decode(pair_codes[ch, i], pair_scale)
            return carry

        lax.fori_loop(0, NB, body, 0)

    def block(p, a, b):
        return 4 * a + b if p == 0 else 4 * b + a

    outer = (along_x, along_z)
    inner = (along_z, along_x)
    part_rows = [slice(p * PART, p * PART + PART) for p in range(2)]
    part_at = [pl.ds(p * PART, PART) for p in range(2)]
    flying = {}

    def b_send(ch):
        for p in range(2):
            peak = jnp.zeros((PART, 128), F32)
            for d in range(1, 4):
                for e in range(4):
                    peak = jnp.maximum(peak, jnp.abs(total[ch, block(p, d, e), part_rows[p]]))
            scale, inverse = scale_of(peak)
            sbp[ch, p] = pack(scale)
            flying["b", ch, p] = []
            for d in range(1, 4):
                for e in range(4):
                    sb[ch, p, d - 1, e] = encode(total[ch, block(p, d, e), part_rows[p]], inverse)
                flying["b", ch, p] += [
                    remote(sb.at[ch, p, d - 1], rb.at[ch, p, d - 1], sem_b.at[ch, p, d - 1], outer[p](d)),
                    remote(sbp.at[ch, p], rbp.at[ch, p, d - 1], sem_b.at[ch, p, d + 2], outer[p](d)),
                ]

    def b_take(ch):
        for p in range(2):
            for copy in flying["b", ch, p]:
                copy.wait()
            scales = [unpack(rbp[ch, p, d], 0, PART) for d in range(3)]
            peak = jnp.zeros((PART, 128), F32)
            for e in range(4):
                at = block(p, 0, e)
                value = total[ch, at, part_rows[p]]
                for d in range(3):
                    value = value + decode(rb[ch, p, d, e], scales[d])
                total[ch, at, part_rows[p]] = value
                if e > 0:
                    peak = jnp.maximum(peak, jnp.abs(value))
            scale, inverse = scale_of(peak)
            scp[ch, p] = pack(scale)
            flying["c", ch, p] = []
            for e in range(1, 4):
                sc[ch, p, e - 1] = encode(total[ch, block(p, 0, e), part_rows[p]], inverse)
                flying["c", ch, p] += [
                    remote(sc.at[ch, p, e - 1], rc.at[ch, p, e - 1], sem_c.at[ch, p, e - 1], inner[p](e)),
                    remote(scp.at[ch, p], rcp.at[ch, p, e - 1], sem_c.at[ch, p, e + 2], inner[p](e)),
                ]

    def c_take(ch):
        for p in range(2):
            for copy in flying["c", ch, p]:
                copy.wait()
            value = total[ch, 0, part_rows[p]]
            for e in range(3):
                value = value + decode(rc[ch, p, e], unpack(rcp[ch, p, e], 0, PART))
            share[ch * HALF + p * PART : ch * HALF + p * PART + PART, :] = value
        mine = share[ch * HALF : ch * HALF + HALF, :]
        scale, inverse = scale_of(jnp.abs(mine))
        gat[ch, x, z, core] = encode(mine, inverse)
        gat_packed[ch, x, z, core] = pack(scale)
        flying["g1", ch] = []
        for d in range(1, 4):
            for p in range(2):
                ref = gat.at[ch, x, z, core, part_at[p]]
                flying["g1", ch].append(remote(ref, ref, sem_g1.at[ch, p, d], inner[p](d)))
            ref = gat_packed.at[ch, x, z, core]
            flying["g1", ch].append(remote(ref, ref, sem_gp1.at[ch, d], inner[0](d)))

    def g1_take(ch):
        for copy in flying["g1", ch]:
            copy.wait()
        flying["g2", ch] = []
        for d in range(1, 4):
            ref = gat.at[ch, x, :, core, part_at[0]]
            flying["g2", ch].append(remote(ref, ref, sem_g2.at[ch, 0, d], along_x(d)))
            ref = gat.at[ch, :, z, core, part_at[1]]
            flying["g2", ch].append(remote(ref, ref, sem_g2.at[ch, 1, d], along_z(d)))
            ref = gat_packed.at[ch, x, :, core]
            flying["g2", ch].append(remote(ref, ref, sem_gp2.at[ch, d], along_x(d)))

    def g2_take(ch):
        for copy in flying["g2", ch]:
            copy.wait()
        ref, packed_ref = gat.at[ch, :, :, core], gat_packed.at[ch, :, :, core]
        flying["f", ch] = [
            remote(ref, ref, sem_f.at[ch], sibling),
            remote(packed_ref, packed_ref, sem_fp.at[ch], sibling),
        ]

    def widen(ch):
        for copy in flying["f", ch]:
            copy.wait()

        def body(i, carry):
            for c in range(2):
                lanes = slice(c * 128, c * 128 + 128)
                scale = unpack(gat_packed[ch, i // 4, i % 4, c], 0, HALF)
                high, low = split(decode(gat[ch, i // 4, i % 4, c], scale))
                s_split[ch, i, :HALF, lanes] = high
                s_split[ch, i, HALF:, lanes] = low
            return carry

        lax.fori_loop(0, NB, body, 0)

    def project(ch):
        prefix[0] = jnp.zeros((HALF, EDGE), F32)

        def body(m, carry):
            for u in range(RUN):
                n = m * RUN + u
                both = nn(s_split[ch, plan[SLOTS + n]], tiles[plan[n]])
                prefix[n + 1] = prefix[n] + (both[:HALF] + both[HALF:])
            return carry

        lax.fori_loop(0, SLOTS // RUN, body, 0)

        def value_of(j):
            return prefix[plan[2 * SLOTS + j + 1]] - prefix[plan[2 * SLOTS + j]]

        def peak_step(j, peak):
            value = jnp.abs(value_of(j))
            return jnp.maximum(peak, jnp.maximum(value[:, :128], value[:, 128:]))

        scale, inverse = scale_of(lax.fori_loop(0, NB, peak_step, jnp.zeros((HALF, 128), F32)))
        p_packed[ch] = pack(scale)

        def code_step(j, carry):
            p_codes[ch, j] = encode(value_of(j), inverse)
            return carry

        lax.fori_loop(0, NB, code_step, 0)

    gens = ((1, 3), (3, 1))
    line = {1: 0, 3: 1}

    def quarter(w):
        return pl.ds(pl.multiple_of(4 * xor2(y, w), 4), 4)

    def y_start(ch, n):
        for h in range(2):
            g, g2 = gens[h]
            w, target = ((2, first_in), (g, second_in))[n]
            flying["a", ch, h, n] = remote(
                p_codes.at[ch, quarter(w), part_at[h]], target.at[ch, h], sem_a.at[ch, h, n], along_y(g)
            )

    def y_first(ch):
        flying["p", ch] = [
            remote(p_packed.at[ch], near_packed.at[ch, n], sem_p.at[ch, n], along_y(g)) for n, g in enumerate((1, 3))
        ]
        y_start(ch, 0)

    def y_second(ch):
        y_start(ch, 1)

    def summed(ch, h, w, takes):
        at = 4 * xor2(y, w)
        own_scale = unpack(p_packed[ch], 10 * h, PART)

        def body(j, peak):
            value = decode(p_codes[ch, at + j, part_rows[h]], own_scale)
            for ref, scale in takes:
                value = value + decode(ref[ch, h, j], scale)
            sums[j] = value
            value = jnp.abs(value)
            return jnp.maximum(peak, jnp.maximum(value[:, :128], value[:, 128:]))

        return lax.fori_loop(0, 4, body, jnp.zeros((PART, 128), F32))

    def near_scale(ch, h):
        return unpack(near_packed[ch, line[gens[h][0]]], 10 * h, PART)

    def y_third(ch):
        for copy in flying["p", ch]:
            copy.wait()
        for h in range(2):
            g, g2 = gens[h]
            flying["a", ch, h, 0].wait()
            scale, inverse = scale_of(summed(ch, h, g2, [(first_in, near_scale(ch, h))]))
            third_packed_out[ch, h] = pack(scale)

            def code(j, carry):
                third_out[ch, h, j] = encode(sums[j], inverse)
                return carry

            lax.fori_loop(0, 4, code, 0)
            flying["3", ch, h] = [
                remote(third_packed_out.at[ch, h], third_packed_in.at[ch, h], sem_3p.at[ch, h], along_y(g2)),
                remote(third_out.at[ch, h], third_in.at[ch, h], sem_3.at[ch, h], along_y(g2)),
            ]

    def send_quarter(ch, h, w, g, n):
        ref = out_codes.at[ch, quarter(w), part_at[h]]
        packed_ref = out_packed.at[xor2(y, w), ch, h]
        flying["q", ch, h, n] = [
            remote(ref, ref, sem_g.at[ch, h, n], along_y(g)),
            remote(packed_ref, packed_ref, sem_gp.at[ch, h, n], along_y(g)),
        ]

    written = []

    def write(ch, h, w):
        at = (ch, quarter(w), part_at[h])
        written.append(pltpu.make_async_copy(out_codes.at[at], result.at[at], sem_out.at[ch, h, w]))
        written[-1].start()

    def y_share(ch):
        for h in range(2):
            g, g2 = gens[h]
            flying["a", ch, h, 1].wait()
            for copy in flying["3", ch, h]:
                copy.wait()
            third_scale = unpack(third_packed_in[ch, h], 0, PART)
            scale, inverse = scale_of(
                summed(ch, h, 0, [(second_in, near_scale(ch, h)), (third_in, third_scale)])
            )
            out_packed[y, ch, h] = pack(scale)

            def code(j, carry):
                out_codes[ch, 4 * y + j, part_rows[h]] = encode(sums[j], inverse)
                return carry

            lax.fori_loop(0, 4, code, 0)
            send_quarter(ch, h, 0, g2, 0)
            send_quarter(ch, h, 0, g, 1)
            write(ch, h, 0)

    def y_pass(ch):
        for h in range(2):
            g, g2 = gens[h]
            for copy in flying["q", ch, h, 0]:
                copy.wait()
            send_quarter(ch, h, g2, g, 2)
            write(ch, h, g2)

    def y_end(ch):
        for h in range(2):
            for n, w in ((1, gens[h][0]), (2, 2)):
                for copy in flying["q", ch, h, n]:
                    copy.wait()
                write(ch, h, w)

    def gram_block():
        mine = me % 20
        tall, wide = mine // 2, mine % 2
        from_ch = tall // 5
        at = pl.multiple_of(32 * (tall % 5), 32)

        def body(m, acc):
            for u in range(4):
                i = 4 * m + u
                a = s_split[from_ch, i, pl.ds(at, 32)]
                b = s_split[from_ch, i, pl.ds(HALF + at, 32)]
                c = s_split[wide, i, :HALF]
                d = s_split[wide, i, HALF:]
                acc = acc + (nt(a, c) + (nt(a, d) + nt(b, c)))
            return acc

        gram_parts[y] = lax.fori_loop(0, NB // 4, body, jnp.zeros((32, HALF), F32))
        ref = gram_parts.at[y]
        flying["y"] = [remote(ref, ref, sem_y.at[d], along_y(d)) for d in range(1, 4)]

    def gram_z():
        for copy in flying["y"]:
            copy.wait()
        gram_all[x, z, core] = (gram_parts[0] + gram_parts[1]) + (gram_parts[2] + gram_parts[3])
        ref = gram_all.at[x, z, core]
        flying["w0"] = [remote(ref, ref, sem_w.at[d], along_z(d)) for d in range(1, 4)]

    def gram_x():
        for copy in flying["w0"]:
            copy.wait()
        ref = gram_all.at[x, :, core]
        flying["w1"] = [remote(ref, ref, sem_w.at[3 + d], along_x(d)) for d in range(1, 4)]

    def gram_pair():
        for copy in flying["w1"]:
            copy.wait()
        ref = gram_all.at[:, :, core]
        flying["w2"] = [remote(ref, ref, sem_w.at[0], sibling)]

    def gram_whole():
        for copy in flying["w2"]:
            copy.wait()
        for tall in range(10):
            for wide in range(2):
                n = 2 * tall + wide
                work[32 * tall : 32 * tall + 32, HALF * wide : HALF * wide + HALF] = gram_all[
                    n // 8, n // 2 % 4, n % 2
                ] * (1.0 / ROWS)
        work[:, K:384] = jnp.zeros((K, 384 - K), F32)
        work[:, 384:] = (
            lax.broadcasted_iota(jnp.int32, (K, 384), 0) == lax.broadcasted_iota(jnp.int32, (K, 384), 1)
        ).astype(F32)

    def eliminate(b):
        top, bottom = b * BLK, b * BLK + BLK
        inverse = pivot_block(work[top:bottom, top:bottom])
        lane, edge = top // 128 * 128, 384 + (bottom + 127) // 128 * 128
        panel = nn(inverse, work[top:bottom, lane:384], precision=HIGHEST)
        known = nn(inverse, work[top:bottom, 384:edge], precision=HIGHEST)
        work[top:bottom, 384:edge] = known
        if bottom < K:
            left = panel[:, bottom - lane : K - lane]
            start = bottom // 128 * 128
            work[bottom:, start:384] -= tn(left, panel[:, start - lane :], precision=HIGHEST)
            work[bottom:, 384:edge] -= tn(left, known, precision=HIGHEST)

    def leave():
        factor[...] = work[:, 384:]

    schedule = [
        (join, 0), (b_send, 0), (join, 1), (load_tiles.start,), (b_take, 0), (c_take, 0), (b_send, 1), (g1_take, 0), (b_take, 1),
        (g2_take, 0), (c_take, 1), (widen, 0), (g1_take, 1), (load_tiles.wait,), (project, 0), (y_first, 0), (y_second, 0),
        (g2_take, 1), (widen, 1), (project, 1), (y_first, 1), (y_third, 0), (gram_block,), (y_second, 1),
        (y_third, 1), (y_share, 0), (gram_z,), (gram_x,), (gram_pair,), (y_share, 1), (y_pass, 0), (gram_whole,),
        (eliminate, 0), (eliminate, 1), (y_pass, 1), (eliminate, 2), (eliminate, 3), (eliminate, 4),
        (leave,), (y_end, 0), (y_end, 1),
    ]
    for stage, *of in schedule:
        stage(*of)
    for copy in written:
        copy.wait()


def final_kernel(codes, packed, share, factor, projected_t, basis_t, left, right):
    step = pl.program_id(0)

    @pl.when(step == 0)
    def _():
        w = factor[:, :K]
        high, low = split(w)
        left[:, :K] = high
        left[:, K : 2 * K] = high
        left[:, 2 * K :] = low
        basis_t[...] = nn(w, share[...], precision=HIGHEST)

    for j in range(FCOLS):
        q = (step * FCOLS + j) // 4
        for ch in range(2):
            scale = jnp.concatenate([unpack(packed[q, ch, 0], 0, PART), unpack(packed[q, ch, 1], 0, PART)], axis=0)
            high, low = split(decode(codes[ch, j], scale))
            at = ch * HALF
            right[at : at + HALF] = high
            right[K + at : K + at + HALF] = low
            right[2 * K + at : 2 * K + at + HALF] = high
        projected_t[:, EDGE * j : EDGE * j + EDGE] = nn(left[...], right[...])


def whole(dims):
    return pl.BlockSpec(dims, lambda *_: (0,) * len(dims))


def vmem(n):
    return [pl.BlockSpec(memory_space=pltpu.VMEM)] * n


def smem(n):
    return [pl.BlockSpec(memory_space=pltpu.SMEM)] * n


def shape(dims, dtype):
    return jax.ShapeDtypeStruct(dims, dtype)


def local(tile_entries, slot_tile_row, slot_tile_column, tile_count, test_matrix):
    anywhere = pl.BlockSpec(memory_space=pl.ANY)
    params = pltpu.CompilerParams(vmem_limit_bytes=VMEM_LIMIT)
    dma = pltpu.SemaphoreType.DMA
    I32 = jnp.int32
    V = pltpu.VMEM

    codes, packed, plan = pl.pallas_call(
        sample_kernel,
        in_specs=smem(3) + [anywhere, anywhere],
        out_specs=[anywhere] + vmem(1) + smem(1),
        out_shape=[
            shape((2, NB, 2, HALF, 128), I16), shape((8, 128), F32),
            shape((2 * SLOTS + NB + 1,), I32),
        ],
        scratch_shapes=[
            V((SLOTS, EDGE, EDGE), BF16), V((K, NB * EDGE), BF16), V((NB + 1, K, EDGE), F32),
            pltpu.SMEM((NB + 1,), I32), V((NB, 2, 2, HALF, 128), I16), dma((GROUPS + 1,)), dma((2, NB)),
        ],
        compiler_params=params,
        name="sample",
    )(slot_tile_row, slot_tile_column, tile_count, tile_entries, test_matrix.T)

    quarters = V((2, 2, 4, PART, EDGE), I16)
    share, out_codes, out_packed, factor = pl.pallas_call(
        main_kernel,
        in_specs=smem(1) + [anywhere] + vmem(1) + [anywhere],
        out_specs=vmem(1) + [anywhere] + vmem(2),
        out_shape=[
            shape((K, 128), F32), shape((2, NB, HALF, EDGE), I16), shape((4, 2, 2, 8, 128), F32), shape((K, 384), F32),
        ],
        scratch_shapes=[
            V((2, NB, HALF, EDGE), I16), V((2, NB, HALF, 128), I16), V((2, NB, HALF, 128), I16), V((8, 128), F32), V((2, NB, HALF, 128), F32),
            V((2, 2, 3, 4, PART, 128), I16), V((2, 2, 3, 4, PART, 128), I16),
            V((2, 2, 3, PART, 128), I16), V((2, 2, 3, PART, 128), I16),
            V((2, 2, 8, 128), F32), V((2, 2, 3, 8, 128), F32),
            V((2, 2, 8, 128), F32), V((2, 2, 3, 8, 128), F32),
            V((2, 4, 4, 2, HALF, 128), I16), V((2, 4, 4, 2, 8, 128), F32),
            V((2, NB, K, EDGE), BF16), V((SLOTS, EDGE, EDGE), BF16), V((SLOTS + 1, HALF, EDGE), F32),
            V((2, NB, HALF, EDGE), I16), V((2, 8, 128), F32),
            quarters, quarters, quarters, quarters, V((4, PART, EDGE), F32),
            V((2, 2, 8, 128), F32), V((2, 2, 8, 128), F32), V((2, 2, 8, 128), F32),
            V((4, 32, HALF), F32), V((4, 4, 2, 32, HALF), F32), V((K, 768), F32),
            dma, dma((2,)), dma((3, 2)), dma((2, 2, 6, 2)), dma((2, 2, 6, 2)),
            dma((2, 2, 4, 2)), dma((2, 2, 4, 2)), dma((2, 4, 2)), dma((2, 4, 2)), dma((2, 2)), dma((2, 2)),
            dma((2, 2, 2, 2)), dma((2, 2, 2)), dma((2, 2, 2)), dma((2, 2, 2)),
            dma((2, 2, 3, 2)), dma((2, 2, 3, 2)), dma((4, 2)), dma((7, 2)), dma((2, 2, 4)),
        ],
        compiler_params=pltpu.CompilerParams(
            vmem_limit_bytes=VMEM_LIMIT, collective_id=0, has_side_effects=True
        ),
        name="plane_and_ring_sums",
    )(plan, codes, packed, tile_entries)

    projected_t, basis_t = pl.pallas_call(
        final_kernel,
        grid=(FSTEPS,),
        in_specs=[
            pl.BlockSpec((2, FCOLS, HALF, EDGE), lambda i: (0, i, 0, 0)),
            whole((4, 2, 2, 8, 128)), whole((K, 128)), whole((K, 384)),
        ],
        out_specs=[pl.BlockSpec((K, FCOLS * EDGE), lambda i: (0, i)), whole((K, 128))],
        out_shape=[shape((K, NB * EDGE), F32), shape((K, 128), F32)],
        scratch_shapes=[V((K, 3 * K), BF16), V((3 * K, EDGE), BF16)],
        compiler_params=params,
        name="final",
    )(out_codes, out_packed, share, factor)
    return (basis_t.T, projected_t.T)


def solution(mesh):
    placed = (
        P(("grp", "col"), None, None),
        P(("grp", "col")),
        P(("grp", "col")),
        P(("grp", "col")),
        P("col", None),
    )
    return jax.shard_map(
        local,
        mesh=mesh,
        in_specs=placed,
        out_specs=(P(("grp", "col"), None), P("col", None)),
        check_vma=False,
    )
```
